32 devices in a mesh: seq: 16 (over z, x, core), head: 2 (over y).
Axes of the slice: x: 2, y: 2, z: 4, core: 2. Of those that a mesh axis runs over, the one named last changes fastest.
Arguments:
- query_rows: bfloat16 [4096, 768], P('seq', 'head'), may hold values from -27 to 27
- key_rows: bfloat16 [4096, 768], P('seq', 'head'), may hold values from -6 to 6
- value_rows: bfloat16 [4096, 768], P('seq', 'head'), may hold values from -6 to 6
- rates: float32 [4096, 4], P('seq', 'head'), may hold values from 0.1 to 1
- fw_decay: float32 [16, 4], P('seq', 'head'), may hold values from 0 to 1
- fw_step: float32 [4], P('head'), may hold values from 0.03 to 0.15
- fast_gate: float32 [4, 192, 384], P('head'), may hold values from -0.4375 to 0.4375
- fast_up: float32 [4, 192, 384], P('head'), may hold values from -0.4375 to 0.4375
- fast_down: float32 [4, 384, 192], P('head'), may hold values from -0.3125 to 0.3125
- ttt_gain: float32 [768], P('head'), may hold values from 0.1 to 1.9
- attn_gain: float32 [768], P('head'), may hold values from 0.1 to 1.9
- out_proj: bfloat16 [768, 768], P('head'), may hold values from -0.21875 to 0.21875
Outputs:
- layer_out: bfloat16 [4096, 768], P(('seq', 'head'))
The draws below stay inside these ranges and needn't reach their ends.
All inputs are finite; a program needn't handle non-finite values.
Results may differ from the reference program's by a relative error of at most 0.0053.
Values may be sent and summed in bfloat16 or wider, within the bound.
A program may use at most 192 MiB of HBM per device.

```python
import math
import jax
import jax.numpy as jnp
from jax import lax

HEAD_DIM = 192
FAST_DIM = 384
BLOCK = 256
WINDOW = 2048
NS_STEPS = 5
ATTN_LANES = 4
WIDTH = 768
SEGMENT_TALLY = 16
SEQLEN = 4096


def paired_rows(key):
    starting_level = jax.random.fold_in(key, 11)
    first_key, second_key = jax.random.split(starting_level, 2)
    queries = jax.random.truncated_normal(first_key, -6.0, 6.0, (SEQLEN, WIDTH), jnp.float32)
    keys_out = jax.random.truncated_normal(second_key, -6.0, 6.0, (SEQLEN, WIDTH), jnp.float32)
    return (queries, keys_out)


def draw_query_rows(key, part):
    return paired_rows(key)[0].astype(jnp.bfloat16)


def draw_key_rows(key, part):
    return paired_rows(key)[1].astype(jnp.bfloat16)


def draw_fw_decay(key, part):
    starting_level = jax.random.fold_in(key, 23)
    diversity_seed, master_seed, dispersion_seed, cluster_seed, loss_target_seed, quick_weight_seed = jax.random.split(starting_level, 6)
    share = 0.5
    slow_heads = jax.random.uniform(diversity_seed, (ATTN_LANES,)) < share
    total_log = jnp.exp(jax.random.uniform(master_seed, (ATTN_LANES,), minval=math.log(0.2), maxval=math.log(1.0)))
    factor = jnp.exp(jax.random.uniform(dispersion_seed, (SEGMENT_TALLY, ATTN_LANES), minval=math.log(0.5), maxval=math.log(2.0)))
    lasting_decay_factor = jnp.exp(-total_log[None, :] * factor / SEGMENT_TALLY)
    fast_keep = jnp.exp(jax.random.uniform(quick_weight_seed, (SEGMENT_TALLY, ATTN_LANES), minval=math.log(0.05), maxval=math.log(0.3)))
    cluster_sets = jax.random.uniform(cluster_seed, (SEGMENT_TALLY, ATTN_LANES)) < 2.0 / SEGMENT_TALLY
    cluster_loss = jax.random.uniform(loss_target_seed, (SEGMENT_TALLY, ATTN_LANES), minval=0.5, maxval=0.8)
    lasting_decay_factor = lasting_decay_factor * jnp.where(cluster_sets, cluster_loss, 1.0)
    return jnp.where(slow_heads[None, :], lasting_decay_factor, fast_keep).astype(jnp.float32)


def level_of(key, shape, cuts, smallest, top_value):
    loudness, own = 1.0, jax.random.fold_in(key, 6)
    for dim, blocks in cuts:
        draws = jnp.exp(jax.random.uniform(jax.random.fold_in(own, dim), (blocks,), jnp.float32, smallest / len(cuts), top_value / len(cuts)))
        loudness = loudness * jnp.repeat(draws, shape[dim] // blocks).reshape([-1 if axis == dim else 1 for axis in range(len(shape))])
    return loudness


def bell_draw(stream_key, shape, scale, most, pieces=(), kind=jnp.bfloat16):
    level = level_of(stream_key, shape, pieces, -0.22, 0.18) if pieces else 1.0
    entries = jax.random.normal(stream_key, shape, jnp.float32) * scale * level
    return jnp.minimum(jnp.maximum(entries, -most), most).astype(kind)


def setup_inputs(seed: int = 0) -> dict:
    arg_keys = jax.random.split(jax.random.key(seed), 13)
    return {
        "query_rows": draw_query_rows(jax.random.fold_in(arg_keys[12], 71), 0),
        "key_rows": draw_key_rows(jax.random.fold_in(arg_keys[12], 71), 0),
        "value_rows": bell_draw(arg_keys[2], (SEQLEN, WIDTH), 1.0, 6.0, ((0, 16), (1, 2))),
        "rates": jnp.clip(jnp.exp(math.log(1.0) - 2.3025851 * jax.random.uniform(arg_keys[3], (SEQLEN, ATTN_LANES), jnp.float32) ** level_of(arg_keys[3], (SEQLEN, ATTN_LANES), ((0, 16), (1, 2)), -0.2, 0.2)), 0.1, 1.0),
        "fw_decay": draw_fw_decay(jax.random.fold_in(arg_keys[12], 71), 0),
        "fw_step": jnp.clip(jnp.exp(math.log(0.15) - 1.609438 * jax.random.uniform(arg_keys[5], (ATTN_LANES,), jnp.float32) ** level_of(arg_keys[5], (ATTN_LANES,), ((0, 2),), -0.2, 0.2)), 0.03, 0.15),
        "fast_gate": bell_draw(arg_keys[6], (ATTN_LANES, HEAD_DIM, FAST_DIM), HEAD_DIM ** -0.5, 0.4375, ((0, 2),), jnp.float32),
        "fast_up": bell_draw(arg_keys[7], (ATTN_LANES, HEAD_DIM, FAST_DIM), HEAD_DIM ** -0.5, 0.4375, ((0, 2),), jnp.float32),
        "fast_down": bell_draw(arg_keys[8], (ATTN_LANES, FAST_DIM, HEAD_DIM), FAST_DIM ** -0.5, 0.3125, ((0, 2),), jnp.float32),
        "ttt_gain": jnp.clip(1.0 + 0.18 * jax.random.normal(arg_keys[9], (WIDTH,), jnp.float32), 0.1, 1.9),
        "attn_gain": jnp.clip(1.0 + 0.18 * jax.random.normal(arg_keys[10], (WIDTH,), jnp.float32), 0.1, 1.9),
        "out_proj": bell_draw(arg_keys[11], (WIDTH, WIDTH), WIDTH ** -0.5, 0.21875, ((0, 2),)),
    }


FULL_PRECISION = lax.Precision.HIGHEST
coef_a = 3.4445
coef_b = -4.775
coef_c = 2.0315

def matmul(left_mat, right_mat):
    return jnp.dot(left_mat, right_mat, precision=FULL_PRECISION, preferred_element_type=jnp.float32)

def rms_rows(values):
    return values * lax.rsqrt(lax.optimization_barrier(jnp.mean(values * values, axis=-1, keepdims=True)) + 1e-06)

def silu_slope(pre_act):
    sigmoid_z = jax.nn.sigmoid(pre_act)
    return sigmoid_z * (1.0 + pre_act * (1.0 - sigmoid_z))

def orthogonalize(gradient):
    current = gradient / (jnp.sqrt(jnp.sum(gradient * gradient)) + 1e-07)
    for sweep_id in range(NS_STEPS):
        gram_mat = matmul(current, current.T)
        poly_mat = coef_b * gram_mat + coef_c * matmul(gram_mat, gram_mat)
        current = coef_a * current + matmul(poly_mat, current)
    return current

def fast_apply(inputs, gate_mat, up_mat, down_mat):
    return matmul(jax.nn.silu(matmul(inputs, gate_mat)) * matmul(inputs, up_mat), down_mat)

def fast_update(key_norm, targets, token_rates, gate_mat, up_mat, down_mat, step_size):
    pre_gate = matmul(key_norm, gate_mat)
    pre_up = matmul(key_norm, up_mat)
    active = jax.nn.silu(pre_gate)
    middle = active * pre_up
    out_grad = -token_rates[:, None] * targets
    grad_down = matmul(middle.T, out_grad)
    mid_grad = matmul(out_grad, down_mat.T)
    grad_gate = matmul(key_norm.T, mid_grad * pre_up * silu_slope(pre_gate))
    grad_up = matmul(key_norm.T, mid_grad * active)
    return (-step_size * orthogonalize(grad_gate), -step_size * orthogonalize(grad_up), -step_size * orthogonalize(grad_down.T).T)

def window_attention(query_head, key_head, value_head, allowed, scale):
    scores = lax.dot_general(query_head, key_head, (((1,), (1,)), ((), ())), preferred_element_type=jnp.float32) * scale
    scores = jnp.where(allowed, scores, -jnp.inf)
    row_max = lax.optimization_barrier(jnp.max(scores, axis=-1, keepdims=True))
    weights = jnp.exp(scores - row_max)
    row_total = lax.optimization_barrier(jnp.sum(weights, axis=-1, keepdims=True))
    return jnp.dot(weights.astype(jnp.bfloat16), value_head, preferred_element_type=jnp.float32) / row_total

def split_heads(rows_mat, head_count):
    return rows_mat.reshape(rows_mat.shape[0], head_count, -1).transpose(1, 0, 2)

def reference(query_rows, key_rows, value_rows, rates, fw_decay, fw_step, fast_gate, fast_up, fast_down, ttt_gain, attn_gain, out_proj):
    scale = 1.0 / math.sqrt(HEAD_DIM)
    key_pad = jnp.concatenate([jnp.zeros((WINDOW, WIDTH), key_rows.dtype), key_rows], axis=0)
    value_pad = jnp.concatenate([jnp.zeros((WINDOW, WIDTH), value_rows.dtype), value_rows], axis=0)
    query_pos = jnp.arange(BLOCK, dtype=jnp.int32)[:, None]
    key_cols = jnp.arange(WINDOW + BLOCK, dtype=jnp.int32)[None, :]
    gain_ttt = ttt_gain.reshape(ATTN_LANES, 1, HEAD_DIM)
    gain_attn = attn_gain.reshape(ATTN_LANES, 1, HEAD_DIM)

    def block_step(states, block_id):
        state_gate, state_up, state_down = states
        start = (block_id * BLOCK).astype(jnp.int32)
        queries = lax.dynamic_slice_in_dim(query_rows, start, BLOCK, 0)
        keys_here = lax.dynamic_slice_in_dim(key_rows, start, BLOCK, 0)
        values_here = lax.dynamic_slice_in_dim(value_rows, start, BLOCK, 0)
        rates_here = lax.dynamic_slice_in_dim(rates, start, BLOCK, 0)
        window_keys = lax.dynamic_slice_in_dim(key_pad, start, WINDOW + BLOCK, 0)
        window_values = lax.dynamic_slice_in_dim(value_pad, start, WINDOW + BLOCK, 0)
        token_pos = start + query_pos
        key_pos = start - WINDOW + key_cols
        allowed = (key_pos <= token_pos) & (key_pos > token_pos - WINDOW) & (key_pos >= 0)
        attended = jax.vmap(window_attention, (0, 0, 0, None, None))(split_heads(queries, ATTN_LANES), split_heads(window_keys, ATTN_LANES), split_heads(window_values, ATTN_LANES), allowed, scale)
        query_norm = rms_rows(split_heads(queries, ATTN_LANES).astype(jnp.float32))
        key_norm = rms_rows(split_heads(keys_here, ATTN_LANES).astype(jnp.float32))
        applied = jax.vmap(fast_apply)(query_norm, fast_gate + state_gate, fast_up + state_up, fast_down + state_down)
        upd_gate, upd_up, upd_down = jax.vmap(fast_update)(key_norm, split_heads(values_here, ATTN_LANES).astype(jnp.float32), rates_here.T, fast_gate, fast_up, fast_down, fw_step)
        retention = fw_decay[block_id][:, None, None]
        new_states = (retention * state_gate + upd_gate, retention * state_up + upd_up, retention * state_down + upd_down)
        mixed = rms_rows(applied) * gain_ttt + rms_rows(attended) * gain_attn
        mixed = mixed.transpose(1, 0, 2).reshape(BLOCK, WIDTH).astype(jnp.bfloat16)
        return (new_states, mixed)
    init = (jnp.zeros((ATTN_LANES, HEAD_DIM, FAST_DIM), jnp.float32), jnp.zeros((ATTN_LANES, HEAD_DIM, FAST_DIM), jnp.float32), jnp.zeros((ATTN_LANES, FAST_DIM, HEAD_DIM), jnp.float32))
    final_states, mixed = lax.scan(block_step, init, jnp.arange(SEGMENT_TALLY, dtype=jnp.int32))
    mixed = mixed.reshape(SEQLEN, WIDTH)
    return jnp.dot(mixed, out_proj, preferred_element_type=jnp.float32).astype(jnp.bfloat16)
```

```python
import functools
import math

import jax
import jax.numpy as jnp
from jax import lax
from jax.experimental import pallas as pl
from jax.experimental.pallas import tpu as pltpu
from jax.sharding import PartitionSpec as P

WINDOW = 2048
NS_STEPS = 5
GROUP = 4
MESH = pl.DeviceIdType.MESH
BF = jnp.bfloat16
F32 = jnp.float32
coef_a = 3.4445
coef_b = -4.775
coef_c = 2.0315
FAR = -1e30

NN = (((1,), (0,)), ((), ()))
NT = (((1,), (1,)), ((), ()))


def dot1(left, right, dims=NN):
    return lax.dot_general(left, right, dims, preferred_element_type=F32)


def halves(value):
    high = value.astype(BF)
    return high, (value - high.astype(F32)).astype(BF)


def dot3(left, right, dims=NN):
    return dot1(left[0], right[0], dims) + (
        dot1(left[0], right[1], dims) + dot1(left[1], right[0], dims)
    )


def rms_rows(values):
    return values * lax.rsqrt(jnp.mean(values * values, axis=-1, keepdims=True) + 1e-06)


def kernel(
    n_seq,
    n_head,
    q_ref,
    k_ref,
    v_ref,
    rates_ref,
    decay_ref,
    step_ref,
    gate_ref,
    up_ref,
    down_ref,
    tgain_ref,
    again_ref,
    proj_ref,
    out_ref,
    kv,
    dec_own,
    dec_sib,
    upd,
    downt,
    x_out,
    x_in,
    s_out,
    s_in,
    h_out,
    h_in,
    state,
    qpad,
    acc,
    top,
    total,
    mixed,
    p_out,
    p_in,
    kv_send,
    kv_recv,
    dec_sems,
    x_send,
    x_recv,
    s_send,
    s_recv,
    h_send,
    h_recv,
    p_send,
    p_recv,
):
    rows = q_ref.shape[0]
    heads, dim, fast = gate_ref.shape
    part = dim // 2
    scale = 1.0 / math.sqrt(dim)
    reach = WINDOW // rows
    n_group = n_seq // GROUP
    n_chip = n_seq // 2
    me = lax.axis_index("seq")
    head = lax.axis_index("head")
    group = me // GROUP
    member = me % GROUP
    side = member // 2
    core = member % 2
    chip = me // 2
    sibling = me + 1 - 2 * core
    across = me + 2 - 4 * side
    onward = me + GROUP
    next_chip = me + 2

    barrier = pltpu.get_barrier_semaphore()

    def greet(seq_pos, head_pos):
        pl.semaphore_signal(barrier, inc=1, device_id=(seq_pos, head_pos), device_id_type=MESH)

    greet(sibling, head)
    greet(across, head)
    expected = jnp.int32(2 + n_head - 1)
    for step in (GROUP, -GROUP, 2, -2):
        there = (me + step >= 0) & (me + step < n_seq)
        pl.when(there)(functools.partial(greet, me + step, head))
        expected = expected + there.astype(jnp.int32)
    for hop in range(1, n_head):
        greet(me, lax.rem(head + hop, n_head))

    own = reach + member
    kv[own, 0] = k_ref[...]
    kv[own, 1] = v_ref[...]
    dec_own[...] = jnp.zeros(dec_own.shape, F32)
    for h in range(heads):
        dec_own[h : h + 1, :] = jnp.broadcast_to(decay_ref[0:1, h : h + 1], (1, 128))
    pl.semaphore_wait(barrier, expected)

    def kv_copy(from_slot, to_slot, number, seq_pos):
        return pltpu.make_async_remote_copy(
            src_ref=kv.at[from_slot],
            dst_ref=kv.at[to_slot],
            send_sem=kv_send.at[number],
            recv_sem=kv_recv.at[to_slot],
            device_id=(seq_pos, head),
            device_id_type=MESH,
        )

    def slot_of(distance):
        return reach + member - distance

    has_next = group + 1 < n_group
    sends = [
        (has_next, own, own - GROUP, 0, onward),
        (side == 0, own, own, 1, across),
        (core == 0, own, own, 2, sibling),
        (has_next & (me >= 4), slot_of(4), slot_of(8), 3, onward),
        (me >= 4, slot_of(4), slot_of(4), 4, across),
        (me >= 4, slot_of(4), slot_of(4), 5, sibling),
        ((me >= 8) & (side == 1), slot_of(8), slot_of(8), 6, across),
        ((me >= 8) & (core == 1), slot_of(8), slot_of(8), 7, sibling),
        (me >= 2, slot_of(2), slot_of(2), 8, sibling),
        (me >= 6, slot_of(6), slot_of(6), 9, sibling),
    ]

    def start_send(number):
        cond, from_slot, to_slot, _, target = sends[number]

        @pl.when(cond)
        def _():
            kv_copy(jnp.maximum(from_slot, 0), jnp.maximum(to_slot, 0), number, target).start()

    def await_block(distance):
        slot = slot_of(distance)
        pltpu.make_async_copy(kv.at[slot], kv.at[slot], kv_recv.at[slot]).wait()

    def arrive(distance, numbers):
        @pl.when(me >= distance)
        def _():
            await_block(distance)
            for number in numbers:
                start_send(number)

    dec_copy = pltpu.make_async_remote_copy(
        src_ref=dec_own,
        dst_ref=dec_sib,
        send_sem=dec_sems.at[0],
        recv_sem=dec_sems.at[1],
        device_id=(sibling, head),
        device_id_type=MESH,
    )
    dec_copy.start()
    for number in (0, 1, 2):
        start_send(number)

    for h in range(heads):
        cols = slice(h * dim, (h + 1) * dim)
        key_norm = rms_rows(k_ref[...].astype(F32)[:, cols])
        err = -rates_ref[:, h : h + 1] * v_ref[...].astype(F32)[:, cols]
        downt[h] = down_ref[h].T
        key_pair = halves(key_norm)
        pre_gate = dot3(key_pair, halves(gate_ref[h]))
        pre_up = dot3(key_pair, halves(up_ref[h]))
        sig = jax.nn.sigmoid(pre_gate)
        active = pre_gate * sig
        back = dot3(halves(err), halves(downt[h]))
        key_t = halves(key_norm.T)
        grads = (
            dot3(key_t, halves(back * pre_up * (sig * (1.0 + pre_gate * (1.0 - sig))))),
            dot3(key_t, halves(back * active)),
            dot3(halves(err.T), halves(active * pre_up)),
        )
        for i, grad in enumerate(grads):
            size = jnp.sum(jnp.sum(grad * grad, axis=1, keepdims=True), axis=0, keepdims=True)
            upd[3 * h + i] = grad / (jnp.sqrt(size) + 1e-07)

    def sweep(turn, carry):
        for j in range(3 * heads):
            current = upd[j]
            low = current.astype(BF)
            gram = dot1(low, low, NT)
            gram_low = gram.astype(BF)
            poly = coef_b * gram + coef_c * dot1(gram_low, gram_low)
            upd[j] = coef_a * current + dot1(poly.astype(BF), low)

        @pl.when(turn == 1)
        def _():
            arrive(4, (3, 4, 5))

        @pl.when(turn == 3)
        def _():
            arrive(2, (8,))

        return carry

    lax.fori_loop(0, NS_STEPS, sweep, 0)

    mine_at = pl.multiple_of(core * part, part)
    other_at = pl.multiple_of((1 - core) * part, part)

    def pair_copy(source, target, send, recv, j, seq_pos):
        return pltpu.make_async_remote_copy(
            src_ref=source.at[j],
            dst_ref=target.at[j],
            send_sem=send.at[j],
            recv_sem=recv.at[j],
            device_id=(seq_pos, head),
            device_id_type=MESH,
        )

    x_copy = lambda j: pair_copy(x_out, x_in, x_send, x_recv, j, sibling)
    s_copy = lambda j: pair_copy(s_out, s_in, s_send, s_recv, j, next_chip)
    h_copy = lambda j: pair_copy(h_out, h_in, h_send, h_recv, j, sibling)

    for j in range(3 * heads):
        h = j // 3
        upd[j] = -step_ref[0:1, h : h + 1] * upd[j]
        x_out[j] = upd[j, pl.ds(other_at, part), :].astype(BF)
        x_copy(j).start()
    dec_copy.wait()

    @pl.when(chip == 0)
    def _():
        s_in[...] = jnp.zeros(s_in.shape, BF)

    arrive(8, (6, 7))
    arrive(6, (9,))

    first = core == 0

    def chain():
        def link(j, carry):
            h = j // 3
            x_copy(j).wait_recv()

            @pl.when(chip > 0)
            def _():
                s_copy(j).wait_recv()

            d_own = dec_own[pl.ds(h, 1), :][:, 0:1]
            d_sib = dec_sib[pl.ds(h, 1), :][:, 0:1]
            decay0 = jnp.where(first, d_own, d_sib)
            decay1 = jnp.where(first, d_sib, d_own)
            u_own = upd[j, pl.ds(mine_at, part), :]
            u_sib = x_in[j].astype(F32)
            u0 = jnp.where(first, u_own, u_sib)
            u1 = jnp.where(first, u_sib, u_own)
            before = s_in[j].astype(F32)
            middle = decay0 * before + u0

            @pl.when(chip + 1 < n_chip)
            def _():
                s_out[j] = (decay1 * middle + u1).astype(BF)
                s_copy(j).start()

            h_out[j] = jnp.where(first, middle, before).astype(BF)
            h_copy(j).start()
            state[j, pl.ds(mine_at, part), :] = jnp.where(first, before, middle)
            return carry

        lax.fori_loop(0, 3 * heads, link, 0)

    lane = lax.broadcasted_iota(jnp.int32, (rows, 256), 1)
    starts = [0, heads * dim - 256]
    for h in range(heads):
        begin = h * dim - starts[h]
        inside = (lane >= begin) & (lane < begin + dim)
        wide = q_ref[:, starts[h] : starts[h] + 256].astype(F32)
        qpad[h] = jnp.where(inside, wide, 0.0).astype(BF)
    acc[...] = jnp.zeros(acc.shape, F32)
    top[...] = jnp.full(top.shape, FAR, F32)
    total[...] = jnp.zeros(total.shape, F32)
    gap = lax.broadcasted_iota(jnp.int32, (rows, rows), 0) - lax.broadcasted_iota(
        jnp.int32, (rows, rows), 1
    )

    def attend(distance, carry):
        @pl.when(2 * chip == distance)
        def _():
            chain()

        @pl.when(me >= distance)
        def _():
            @pl.when(distance % 2 == 1)
            def _():
                await_block(distance)

            slot = slot_of(distance)
            back = gap + distance * rows
            allowed = (back >= 0) & (back < WINDOW)
            for h in range(heads):
                cols = slice(starts[h], starts[h] + 256)
                scores = dot1(qpad[h], kv[slot, 0, :, cols], NT) * scale
                scores = jnp.where(allowed, scores, FAR)
                old_top = top[h][:, 0:1]
                new_top = jnp.maximum(old_top, jnp.max(scores, axis=1, keepdims=True))
                weights = jnp.exp(scores - new_top)
                shrink = jnp.exp(old_top - new_top)
                total[h] = jnp.broadcast_to(
                    total[h][:, 0:1] * shrink + jnp.sum(weights, axis=1, keepdims=True), (rows, 128)
                )
                acc[h] = acc[h] * shrink + dot1(weights.astype(BF), kv[slot, 1, :, cols])
                top[h] = jnp.broadcast_to(new_top, (rows, 128))

        return carry

    lax.fori_loop(0, reach + 1, attend, 0)

    @pl.when(2 * chip > reach)
    def _():
        chain()

    for j in range(3 * heads):
        h_copy(j).wait_recv()
        state[j, pl.ds(other_at, part), :] = h_in[j].astype(F32)

    for h in range(heads):
        cols = slice(h * dim, (h + 1) * dim)
        query = halves(rms_rows(q_ref[...].astype(F32)[:, cols]))
        pre_gate = dot3(query, halves(gate_ref[h] + state[3 * h]))
        pre_up = dot3(query, halves(up_ref[h] + state[3 * h + 1]))
        hidden = pre_gate * jax.nn.sigmoid(pre_gate) * pre_up
        applied = dot3(halves(hidden), halves(downt[h] + state[3 * h + 2]), NT)
        begin = h * dim - starts[h]
        attended = acc[h][:, begin : begin + dim] / total[h][:, 0:1]
        mixed[h] = (
            rms_rows(applied) * tgain_ref[...][:, cols]
            + rms_rows(attended) * again_ref[...][:, cols]
        ).astype(BF)

    share = rows // n_head

    def project(target):
        at = pl.multiple_of(target * share, share)
        result = dot1(mixed[0, pl.ds(at, share), :], proj_ref[0:dim, :])
        for h in range(1, heads):
            result = result + dot1(
                mixed[h, pl.ds(at, share), :], proj_ref[h * dim : (h + 1) * dim, :]
            )
        return result

    def p_copy(hop):
        return pltpu.make_async_remote_copy(
            src_ref=p_out.at[hop - 1],
            dst_ref=p_in.at[hop - 1],
            send_sem=p_send.at[hop - 1],
            recv_sem=p_recv.at[hop - 1],
            device_id=(me, lax.rem(head + hop, n_head)),
            device_id_type=MESH,
        )

    for hop in range(1, n_head):
        p_out[hop - 1] = project(lax.rem(head + hop, n_head)).astype(BF)
        p_copy(hop).start()
    result = project(head)
    for hop in range(1, n_head):
        p_copy(hop).wait_recv()
        result = result + p_in[hop - 1].astype(F32)
    out_ref[...] = result.astype(BF)

    for number, (cond, from_slot, to_slot, _, target) in enumerate(sends):

        @pl.when(cond)
        def _():
            kv_copy(
                jnp.maximum(from_slot, 0), jnp.maximum(to_slot, 0), number, target
            ).wait_send()

    for j in range(3 * heads):
        x_copy(j).wait_send()
        h_copy(j).wait_send()

        @pl.when(chip + 1 < n_chip)
        def _():
            s_copy(j).wait_send()

    for hop in range(1, n_head):
        p_copy(hop).wait_send()


def local(
    n_seq,
    n_head,
    query_rows,
    key_rows,
    value_rows,
    rates,
    fw_decay,
    fw_step,
    fast_gate,
    fast_up,
    fast_down,
    ttt_gain,
    attn_gain,
    out_proj,
):
    rows, cols = query_rows.shape
    heads, dim, fast = fast_gate.shape
    width = out_proj.shape[1]
    share = rows // n_head
    mats = 3 * heads
    part = dim // 2
    slots = WINDOW // rows + GROUP
    dma = pltpu.SemaphoreType.DMA
    piece = pltpu.VMEM((mats, part, fast), BF)
    return pl.pallas_call(
        functools.partial(kernel, n_seq, n_head),
        out_shape=jax.ShapeDtypeStruct((share, width), BF),
        in_specs=[pl.BlockSpec(memory_space=pltpu.VMEM)] * 12,
        out_specs=pl.BlockSpec(memory_space=pltpu.VMEM),
        scratch_shapes=[
            pltpu.VMEM((slots, 2, rows, cols), BF),
            pltpu.VMEM((8, 128), F32),
            pltpu.VMEM((8, 128), F32),
            pltpu.VMEM((mats, dim, fast), F32),
            pltpu.VMEM((heads, dim, fast), F32),
            piece,
            piece,
            piece,
            piece,
            piece,
            piece,
            pltpu.VMEM((mats, dim, fast), F32),
            pltpu.VMEM((heads, rows, 256), BF),
            pltpu.VMEM((heads, rows, 256), F32),
            pltpu.VMEM((heads, rows, 128), F32),
            pltpu.VMEM((heads, rows, 128), F32),
            pltpu.VMEM((heads, rows, dim), BF),
            pltpu.VMEM((n_head - 1, share, width), BF),
            pltpu.VMEM((n_head - 1, share, width), BF),
            dma((10,)),
            dma((slots,)),
            dma((2,)),
            dma((mats,)),
            dma((mats,)),
            dma((mats,)),
            dma((mats,)),
            dma((mats,)),
            dma((mats,)),
            dma((n_head - 1,)),
            dma((n_head - 1,)),
        ],
        compiler_params=pltpu.CompilerParams(
            collective_id=0, has_side_effects=True, vmem_limit_bytes=48 * 1024 * 1024
        ),
    )(
        query_rows,
        key_rows,
        value_rows,
        rates,
        fw_decay,
        fw_step.reshape(1, -1),
        fast_gate,
        fast_up,
        fast_down,
        ttt_gain.reshape(1, -1),
        attn_gain.reshape(1, -1),
        out_proj,
    )


def solution(mesh):
    in_specs = (
        P("seq", "head"),
        P("seq", "head"),
        P("seq", "head"),
        P("seq", "head"),
        P("seq", "head"),
        P("head"),
        P("head", None, None),
        P("head", None, None),
        P("head", None, None),
        P("head"),
        P("head"),
        P("head", None),
    )
    out_specs = P(("seq", "head"), None)
    body = functools.partial(local, mesh.shape["seq"], mesh.shape["head"])
    return jax.shard_map(body, mesh=mesh, in_specs=in_specs, out_specs=out_specs, check_vma=False)
```

```python
import functools
import math

import jax
import jax.numpy as jnp
from jax import lax
from jax.experimental import pallas as pl
from jax.experimental.pallas import tpu as pltpu
from jax.sharding import PartitionSpec as P

WINDOW = 2048
NS_STEPS = 5
GROUP = 4
SPLIT = 2
MESH = pl.DeviceIdType.MESH
BF = jnp.bfloat16
F32 = jnp.float32
coef_a = 3.4445
coef_b = -4.775
coef_c = 2.0315
FAR = -1e30

NN = (((1,), (0,)), ((), ()))
NT = (((1,), (1,)), ((), ()))


def dot1(left, right, dims=NN):
    return lax.dot_general(left, right, dims, preferred_element_type=F32)


def halves(value):
    high = value.astype(BF)
    return high, (value - high.astype(F32)).astype(BF)


def dot3(left, right, dims=NN):
    return dot1(left[0], right[0], dims) + (
        dot1(left[0], right[1], dims) + dot1(left[1], right[0], dims)
    )


def rms_rows(values):
    return values * lax.rsqrt(jnp.mean(values * values, axis=-1, keepdims=True) + 1e-06)


def kernel(
    n_seq,
    n_head,
    q_hbm,
    k_hbm,
    v_hbm,
    rates_ref,
    decay_ref,
    step_ref,
    gate_hbm,
    up_hbm,
    downt_hbm,
    tgain_ref,
    again_ref,
    proj_hbm,
    out_ref,
    q_ref,
    gate_ref,
    up_ref,
    downt,
    proj_ref,
    kv,
    dec_own,
    dec_sib,
    dec_chip,
    dec_across,
    upd,
    x_out,
    x_in,
    t_own,
    t_out,
    t_in,
    s_out,
    s_in,
    h_out,
    h_in,
    state,
    qpad,
    acc,
    top,
    total,
    mixed,
    p_out,
    p_in,
    load_sems,
    kv_send,
    kv_recv,
    dec_sems,
    x_send,
    x_recv,
    t_send,
    t_recv,
    s_send,
    s_recv,
    h_send,
    h_recv,
    p_send,
    p_recv,
):
    rows = q_ref.shape[0]
    heads, dim, _ = gate_ref.shape
    part = dim // 2
    chunk = part // SPLIT
    pieces = 3 * heads * SPLIT
    scale = 1.0 / math.sqrt(dim)
    reach = WINDOW // rows
    n_group = n_seq // GROUP
    me = lax.axis_index("seq")
    head = lax.axis_index("head")
    group = me // GROUP
    member = me % GROUP
    side = member // 2
    core = member % 2
    sibling = me + 1 - 2 * core
    across = me + 2 - 4 * side
    onward = me + GROUP
    own = reach + member

    loads = [
        pltpu.make_async_copy(source, target, load_sems.at[i])
        for i, (source, target) in enumerate(
            (
                (k_hbm, kv.at[own, 0]),
                (v_hbm, kv.at[own, 1]),
                (gate_hbm, gate_ref),
                (up_hbm, up_ref),
                (downt_hbm, downt),
                (q_hbm, q_ref),
                (proj_hbm, proj_ref),
            )
        )
    ]
    for load in loads:
        load.start()

    barrier = pltpu.get_barrier_semaphore()

    def greet(seq_pos, head_pos):
        pl.semaphore_signal(barrier, inc=1, device_id=(seq_pos, head_pos), device_id_type=MESH)

    greet(sibling, head)
    greet(across, head)
    expected = jnp.int32(2 + n_head - 1)
    for step in (GROUP, -GROUP):
        there = (me + step >= 0) & (me + step < n_seq)
        pl.when(there)(functools.partial(greet, me + step, head))
        expected = expected + there.astype(jnp.int32)
    for hop in range(1, n_head):
        greet(me, lax.rem(head + hop, n_head))

    dec_own[...] = jnp.zeros(dec_own.shape, F32)
    for h in range(heads):
        dec_own[h : h + 1, :] = jnp.broadcast_to(decay_ref[0:1, h : h + 1], (1, 128))
    loads[0].wait()
    loads[1].wait()
    pl.semaphore_wait(barrier, expected)

    def kv_copy(from_slot, to_slot, number, seq_pos):
        return pltpu.make_async_remote_copy(
            src_ref=kv.at[from_slot],
            dst_ref=kv.at[to_slot],
            send_sem=kv_send.at[number],
            recv_sem=kv_recv.at[to_slot],
            device_id=(seq_pos, head),
            device_id_type=MESH,
        )

    def slot_of(distance):
        return reach + member - distance

    has_next = group + 1 < n_group
    sends = [
        (has_next, own, own - GROUP, 0, onward),
        (side == 0, own, own, 1, across),
        (core == 0, own, own, 2, sibling),
        (has_next & (me >= 4), slot_of(4), slot_of(8), 3, onward),
        (me >= 4, slot_of(4), slot_of(4), 4, across),
        (me >= 4, slot_of(4), slot_of(4), 5, sibling),
        ((me >= 8) & (side == 1), slot_of(8), slot_of(8), 6, across),
        ((me >= 8) & (core == 1), slot_of(8), slot_of(8), 7, sibling),
        (me >= 2, slot_of(2), slot_of(2), 8, sibling),
        (me >= 6, slot_of(6), slot_of(6), 9, sibling),
    ]

    def start_send(number):
        cond, from_slot, to_slot, _, target = sends[number]

        @pl.when(cond)
        def _():
            kv_copy(jnp.maximum(from_slot, 0), jnp.maximum(to_slot, 0), number, target).start()

    def await_block(distance):
        slot = slot_of(distance)
        pltpu.make_async_copy(kv.at[slot], kv.at[slot], kv_recv.at[slot]).wait()

    def arrive(distance, numbers):
        @pl.when(me >= distance)
        def _():
            await_block(distance)
            for number in numbers:
                start_send(number)

    dec_copy = pltpu.make_async_remote_copy(
        src_ref=dec_own,
        dst_ref=dec_sib,
        send_sem=dec_sems.at[0],
        recv_sem=dec_sems.at[1],
        device_id=(sibling, head),
        device_id_type=MESH,
    )
    dec_copy.start()
    for number in (0, 1, 2):
        start_send(number)

    for load in loads[2:5]:
        load.wait()

    for h in range(heads):
        cols = slice(h * dim, (h + 1) * dim)
        key_norm = rms_rows(kv[own, 0].astype(F32)[:, cols])
        rate = jnp.broadcast_to(rates_ref[h : h + 1, :], (8, rows)).T[:, 0:1]
        err = -rate * kv[own, 1].astype(F32)[:, cols]
        key_pair = halves(key_norm)
        pre_gate = dot3(key_pair, halves(gate_ref[h]))
        pre_up = dot3(key_pair, halves(up_ref[h]))
        sig = jax.nn.sigmoid(pre_gate)
        active = pre_gate * sig
        back = dot3(halves(err), halves(downt[h]))
        key_t = halves(key_norm.T)
        grads = (
            dot3(key_t, halves(back * pre_up * (sig * (1.0 + pre_gate * (1.0 - sig))))),
            dot3(key_t, halves(back * active)),
            dot3(halves(err.T), halves(active * pre_up)),
        )
        for i, grad in enumerate(grads):
            size = jnp.sum(jnp.sum(grad * grad, axis=1, keepdims=True), axis=0, keepdims=True)
            upd[3 * h + i] = grad / (jnp.sqrt(size) + 1e-07)

    def sweep(turn, carry):
        for j in range(3 * heads):
            current = upd[j]
            low = current.astype(BF)
            gram = dot1(low, low, NT)
            gram_low = gram.astype(BF)
            poly = coef_b * gram + coef_c * dot1(gram_low, gram_low)
            upd[j] = coef_a * current + dot1(poly.astype(BF), low)

        @pl.when(turn == 1)
        def _():
            arrive(4, (3, 4, 5))

        @pl.when(turn == 3)
        def _():
            arrive(2, (8,))

        return carry

    lax.fori_loop(0, NS_STEPS, sweep, 0)

    mine_at = pl.multiple_of(core * part, part)
    other_at = pl.multiple_of((1 - core) * part, part)

    def pair_copy(source, target, send, recv, j, seq_pos):
        return pltpu.make_async_remote_copy(
            src_ref=source.at[j],
            dst_ref=target.at[j],
            send_sem=send.at[j],
            recv_sem=recv.at[j],
            device_id=(seq_pos, head),
            device_id_type=MESH,
        )

    x_copy = lambda p: pair_copy(x_out, x_in, x_send, x_recv, p, sibling)
    t_copy = lambda p: pair_copy(t_out, t_in, t_send, t_recv, p, across)
    s_copy = lambda p: pair_copy(s_out, s_in, s_send, s_recv, p, onward)
    h_copy = lambda p: pair_copy(h_out, h_in, h_send, h_recv, p, sibling)

    def rows_at(p, base):
        return pl.ds(pl.multiple_of(base + (p % SPLIT) * chunk, chunk), chunk)

    for p in range(pieces):
        j = p // SPLIT
        if p % SPLIT == 0:
            upd[j] = -step_ref[0:1, j // 3 : j // 3 + 1] * upd[j]
        x_out[p] = upd[j, rows_at(p, other_at), :].astype(BF)
        x_copy(p).start()
    dec_copy.wait()
    dec_chip[...] = dec_own[...] * dec_sib[...]
    dec_chip_copy = pltpu.make_async_remote_copy(
        src_ref=dec_chip,
        dst_ref=dec_across,
        send_sem=dec_sems.at[2],
        recv_sem=dec_sems.at[3],
        device_id=(across, head),
        device_id_type=MESH,
    )
    dec_chip_copy.start()

    @pl.when(group == 0)
    def _():
        s_in[...] = jnp.zeros(s_in.shape, BF)

    first = core == 0

    def of_pair(p):
        j = p // SPLIT
        h = j // 3
        d_own = dec_own[pl.ds(h, 1), :][:, 0:1]
        d_sib = dec_sib[pl.ds(h, 1), :][:, 0:1]
        u_own = upd[j, rows_at(p, mine_at), :]
        u_sib = x_in[p].astype(F32)
        return (
            jnp.where(first, d_own, d_sib),
            jnp.where(first, d_sib, d_own),
            jnp.where(first, u_own, u_sib),
            jnp.where(first, u_sib, u_own),
        )

    def sum_pair(p, carry):
        x_copy(p).wait_recv()
        _, decay1, u0, u1 = of_pair(p)
        both = decay1 * u0 + u1
        t_own[p] = both
        t_out[p] = both.astype(BF)
        t_copy(p).start()
        return carry

    lax.fori_loop(0, pieces, sum_pair, 0)
    dec_chip_copy.wait()

    arrive(8, (6, 7))
    arrive(6, (9,))

    near = side == 0

    def chain():
        def link(p, carry):
            h = p // SPLIT // 3
            t_copy(p).wait_recv()

            @pl.when(group > 0)
            def _():
                s_copy(p).wait_recv()

            c_own = dec_chip[pl.ds(h, 1), :][:, 0:1]
            c_far = dec_across[pl.ds(h, 1), :][:, 0:1]
            chip0 = jnp.where(near, c_own, c_far)
            chip1 = jnp.where(near, c_far, c_own)
            t_far = t_in[p].astype(F32)
            t_mine = t_own[p]
            t0 = jnp.where(near, t_mine, t_far)
            t1 = jnp.where(near, t_far, t_mine)
            enter = s_in[p].astype(F32)
            halfway = chip0 * enter + t0

            @pl.when(has_next)
            def _():
                s_out[p] = (chip1 * halfway + t1).astype(BF)
                s_copy(p).start()

            decay0, _, u0, _ = of_pair(p)
            before = jnp.where(near, enter, halfway)
            middle = decay0 * before + u0
            h_out[p] = jnp.where(first, middle, before).astype(BF)
            h_copy(p).start()
            state[p // SPLIT, rows_at(p, mine_at), :] = jnp.where(first, before, middle)
            return carry

        lax.fori_loop(0, pieces, link, 0)

    loads[5].wait()
    lane = lax.broadcasted_iota(jnp.int32, (rows, 256), 1)
    starts = [0, heads * dim - 256]
    for h in range(heads):
        begin = h * dim - starts[h]
        inside = (lane >= begin) & (lane < begin + dim)
        wide = q_ref[:, starts[h] : starts[h] + 256].astype(F32)
        qpad[h] = jnp.where(inside, wide, 0.0).astype(BF)
    acc[...] = jnp.zeros(acc.shape, F32)
    top[...] = jnp.full(top.shape, FAR, F32)
    total[...] = jnp.zeros(total.shape, F32)
    gap = lax.broadcasted_iota(jnp.int32, (rows, rows), 0) - lax.broadcasted_iota(
        jnp.int32, (rows, rows), 1
    )

    def attend(distance, carry):
        @pl.when(3 * group == distance)
        def _():
            chain()

        @pl.when(me >= distance)
        def _():
            @pl.when(distance % 2 == 1)
            def _():
                await_block(distance)

            slot = slot_of(distance)
            back = gap + distance * rows
            allowed = (back >= 0) & (back < WINDOW)
            for h in range(heads):
                cols = slice(starts[h], starts[h] + 256)
                scores = dot1(qpad[h], kv[slot, 0, :, cols], NT) * scale
                scores = jnp.where(allowed, scores, FAR)
                old_top = top[h][:, 0:1]
                new_top = jnp.maximum(old_top, jnp.max(scores, axis=1, keepdims=True))
                weights = jnp.exp(scores - new_top)
                shrink = jnp.exp(old_top - new_top)
                total[h] = jnp.broadcast_to(
                    total[h][:, 0:1] * shrink + jnp.sum(weights, axis=1, keepdims=True), (rows, 128)
                )
                acc[h] = acc[h] * shrink + dot1(weights.astype(BF), kv[slot, 1, :, cols])
                top[h] = jnp.broadcast_to(new_top, (rows, 128))

        return carry

    lax.fori_loop(0, reach + 1, attend, 0)

    @pl.when(3 * group > reach)
    def _():
        chain()

    loads[6].wait()
    for p in range(pieces):
        h_copy(p).wait_recv()
        state[p // SPLIT, rows_at(p, other_at), :] = h_in[p].astype(F32)

    for h in range(heads):
        cols = slice(h * dim, (h + 1) * dim)
        query = halves(rms_rows(q_ref[...].astype(F32)[:, cols]))
        pre_gate = dot3(query, halves(gate_ref[h] + state[3 * h]))
        pre_up = dot3(query, halves(up_ref[h] + state[3 * h + 1]))
        hidden = pre_gate * jax.nn.sigmoid(pre_gate) * pre_up
        applied = dot3(halves(hidden), halves(downt[h] + state[3 * h + 2]), NT)
        begin = h * dim - starts[h]
        attended = acc[h][:, begin : begin + dim] / total[h][:, 0:1]
        mixed[h] = (
            rms_rows(applied) * tgain_ref[...].reshape(1, -1)[:, cols]
            + rms_rows(attended) * again_ref[...].reshape(1, -1)[:, cols]
        ).astype(BF)

    share = rows // n_head

    def project(target):
        at = pl.multiple_of(target * share, share)
        result = dot1(mixed[0, pl.ds(at, share), :], proj_ref[0:dim, :])
        for h in range(1, heads):
            result = result + dot1(
                mixed[h, pl.ds(at, share), :], proj_ref[h * dim : (h + 1) * dim, :]
            )
        return result

    def p_copy(hop):
        return pltpu.make_async_remote_copy(
            src_ref=p_out.at[hop - 1],
            dst_ref=p_in.at[hop - 1],
            send_sem=p_send.at[hop - 1],
            recv_sem=p_recv.at[hop - 1],
            device_id=(me, lax.rem(head + hop, n_head)),
            device_id_type=MESH,
        )

    for hop in range(1, n_head):
        p_out[hop - 1] = project(lax.rem(head + hop, n_head)).astype(BF)
        p_copy(hop).start()
    result = project(head)
    for hop in range(1, n_head):
        p_copy(hop).wait_recv()
        result = result + p_in[hop - 1].astype(F32)
    out_ref[...] = result.astype(BF)

    for number, (cond, from_slot, to_slot, _, target) in enumerate(sends):

        @pl.when(cond)
        def _():
            kv_copy(
                jnp.maximum(from_slot, 0), jnp.maximum(to_slot, 0), number, target
            ).wait_send()

    for p in range(pieces):
        x_copy(p).wait_send()
        t_copy(p).wait_send()
        h_copy(p).wait_send()

        @pl.when(has_next)
        def _():
            s_copy(p).wait_send()

    for hop in range(1, n_head):
        p_copy(hop).wait_send()


def local(
    n_seq,
    n_head,
    query_rows,
    key_rows,
    value_rows,
    rates,
    fw_decay,
    fw_step,
    fast_gate,
    fast_up,
    fast_down,
    ttt_gain,
    attn_gain,
    out_proj,
):
    rows, cols = query_rows.shape
    heads, dim, fast = fast_gate.shape
    width = out_proj.shape[1]
    share = rows // n_head
    mats = 3 * heads
    slots = WINDOW // rows + GROUP
    dma = pltpu.SemaphoreType.DMA
    pieces = mats * SPLIT
    chunk = dim // 2 // SPLIT
    piece = pltpu.VMEM((pieces, chunk, fast), BF)
    moved = pl.BlockSpec(memory_space=pl.ANY)
    small = pl.BlockSpec(memory_space=pltpu.VMEM)
    return pl.pallas_call(
        functools.partial(kernel, n_seq, n_head),
        out_shape=jax.ShapeDtypeStruct((share, width), BF),
        in_specs=[moved] * 3 + [small] * 3 + [moved] * 3 + [small] * 2 + [moved],
        out_specs=pl.BlockSpec(memory_space=pltpu.VMEM),
        scratch_shapes=[
            pltpu.VMEM((rows, cols), BF),
            pltpu.VMEM((heads, dim, fast), F32),
            pltpu.VMEM((heads, dim, fast), F32),
            pltpu.VMEM((heads, dim, fast), F32),
            pltpu.VMEM((cols, width), BF),
            pltpu.VMEM((slots, 2, rows, cols), BF),
            pltpu.VMEM((8, 128), F32),
            pltpu.VMEM((8, 128), F32),
            pltpu.VMEM((8, 128), F32),
            pltpu.VMEM((8, 128), F32),
            pltpu.VMEM((mats, dim, fast), F32),
            piece,
            piece,
            pltpu.VMEM((pieces, chunk, fast), F32),
            piece,
            piece,
            piece,
            piece,
            piece,
            piece,
            pltpu.VMEM((mats, dim, fast), F32),
            pltpu.VMEM((heads, rows, 256), BF),
            pltpu.VMEM((heads, rows, 256), F32),
            pltpu.VMEM((heads, rows, 128), F32),
            pltpu.VMEM((heads, rows, 128), F32),
            pltpu.VMEM((heads, rows, dim), BF),
            pltpu.VMEM((n_head - 1, share, width), BF),
            pltpu.VMEM((n_head - 1, share, width), BF),
            dma((7,)),
            dma((10,)),
            dma((slots,)),
            dma((4,)),
            dma((pieces,)),
            dma((pieces,)),
            dma((pieces,)),
            dma((pieces,)),
            dma((pieces,)),
            dma((pieces,)),
            dma((pieces,)),
            dma((pieces,)),
            dma((n_head - 1,)),
            dma((n_head - 1,)),
        ],
        compiler_params=pltpu.CompilerParams(
            collective_id=0, has_side_effects=True, vmem_limit_bytes=56 * 1024 * 1024
        ),
    )(
        query_rows,
        key_rows,
        value_rows,
        rates.T,
        fw_decay,
        fw_step.reshape(1, -1),
        fast_gate,
        fast_up,
        jnp.swapaxes(fast_down, 1, 2),
        ttt_gain,
        attn_gain,
        out_proj,
    )


def solution(mesh):
    in_specs = (
        P("seq", "head"),
        P("seq", "head"),
        P("seq", "head"),
        P("seq", "head"),
        P("seq", "head"),
        P("head"),
        P("head", None, None),
        P("head", None, None),
        P("head", None, None),
        P("head"),
        P("head"),
        P("head", None),
    )
    out_specs = P(("seq", "head"), None)
    body = functools.partial(local, mesh.shape["seq"], mesh.shape["head"])
    return jax.shard_map(body, mesh=mesh, in_specs=in_specs, out_specs=out_specs, check_vma=False)
```

```python
import functools
import math

import jax
import jax.numpy as jnp
from jax import lax
from jax.experimental import pallas as pl
from jax.experimental.pallas import tpu as pltpu
from jax.sharding import PartitionSpec as P

WINDOW = 2048
NS_STEPS = 5
GROUP = 4
SPLIT = 2
MESH = pl.DeviceIdType.MESH
BF = jnp.bfloat16
F32 = jnp.float32
coef_a = 3.4445
coef_b = -4.775
coef_c = 2.0315
FAR = -1e30

NN = (((1,), (0,)), ((), ()))
NT = (((1,), (1,)), ((), ()))


def dot1(left, right, dims=NN):
    return lax.dot_general(left, right, dims, preferred_element_type=F32)


def halves(value):
    high = value.astype(BF)
    return high, (value - high.astype(F32)).astype(BF)


def dot3(left, right, dims=NN):
    return dot1(left[0], right[0], dims) + (
        dot1(left[0], right[1], dims) + dot1(left[1], right[0], dims)
    )


def rms_rows(values):
    return values * lax.rsqrt(jnp.mean(values * values, axis=-1, keepdims=True) + 1e-06)


def kernel(
    n_seq,
    n_head,
    q_hbm,
    k_hbm,
    v_hbm,
    rates_ref,
    decay_ref,
    step_ref,
    gate_hbm,
    up_hbm,
    downt_hbm,
    tgain_ref,
    again_ref,
    proj_hbm,
    out_ref,
    q_ref,
    gate_ref,
    up_ref,
    downt,
    proj_ref,
    kv,
    dec_own,
    dec_sib,
    dec_chip,
    dec_across,
    upd,
    x_out,
    x_in,
    t_own,
    t_out,
    t_in,
    s_out,
    s_in,
    h_out,
    h_in,
    state,
    qpad,
    acc,
    top,
    total,
    share_attn,
    query_pair,
    mixed,
    p_out,
    p_in,
    load_sems,
    kv_send,
    kv_recv,
    dec_sems,
    x_send,
    x_recv,
    t_send,
    t_recv,
    s_send,
    s_recv,
    h_send,
    h_recv,
    p_send,
    p_recv,
):
    rows = q_ref.shape[0]
    heads, dim, _ = gate_ref.shape
    part = dim // 2
    chunk = part // SPLIT
    pieces = 3 * heads * SPLIT
    scale = 1.0 / math.sqrt(dim)
    reach = WINDOW // rows
    n_group = n_seq // GROUP
    me = lax.axis_index("seq")
    head = lax.axis_index("head")
    group = me // GROUP
    member = me % GROUP
    side = member // 2
    core = member % 2
    sibling = me + 1 - 2 * core
    across = me + 2 - 4 * side
    onward = me + GROUP
    own = reach + member

    loads = [
        pltpu.make_async_copy(source, target, load_sems.at[i])
        for i, (source, target) in enumerate(
            (
                (k_hbm, kv.at[own, 0]),
                (v_hbm, kv.at[own, 1]),
                (gate_hbm, gate_ref),
                (up_hbm, up_ref),
                (downt_hbm, downt),
                (q_hbm, q_ref),
                (proj_hbm, proj_ref),
            )
        )
    ]
    for load in loads:
        load.start()

    barrier = pltpu.get_barrier_semaphore()

    def greet(seq_pos, head_pos):
        pl.semaphore_signal(barrier, inc=1, device_id=(seq_pos, head_pos), device_id_type=MESH)

    greet(sibling, head)
    greet(across, head)
    expected = jnp.int32(2 + n_head - 1)
    for step in (GROUP, -GROUP):
        there = (me + step >= 0) & (me + step < n_seq)
        pl.when(there)(functools.partial(greet, me + step, head))
        expected = expected + there.astype(jnp.int32)
    for hop in range(1, n_head):
        greet(me, lax.rem(head + hop, n_head))

    dec_own[...] = jnp.zeros(dec_own.shape, F32)
    for h in range(heads):
        dec_own[h : h + 1, :] = jnp.broadcast_to(decay_ref[0:1, h : h + 1], (1, 128))
    loads[0].wait()
    loads[1].wait()
    pl.semaphore_wait(barrier, expected)

    def kv_copy(from_slot, to_slot, number, seq_pos):
        return pltpu.make_async_remote_copy(
            src_ref=kv.at[from_slot],
            dst_ref=kv.at[to_slot],
            send_sem=kv_send.at[number],
            recv_sem=kv_recv.at[to_slot],
            device_id=(seq_pos, head),
            device_id_type=MESH,
        )

    def slot_of(distance):
        return reach + member - distance

    has_next = group + 1 < n_group
    sends = [
        (has_next, own, own - GROUP, 0, onward),
        (side == 0, own, own, 1, across),
        (core == 0, own, own, 2, sibling),
        (has_next & (me >= 4), slot_of(4), slot_of(8), 3, onward),
        (me >= 4, slot_of(4), slot_of(4), 4, across),
        (me >= 4, slot_of(4), slot_of(4), 5, sibling),
        ((me >= 8) & (side == 1), slot_of(8), slot_of(8), 6, across),
        ((me >= 8) & (core == 1), slot_of(8), slot_of(8), 7, sibling),
        (me >= 2, slot_of(2), slot_of(2), 8, sibling),
        (me >= 6, slot_of(6), slot_of(6), 9, sibling),
    ]

    def start_send(number):
        cond, from_slot, to_slot, _, target = sends[number]

        @pl.when(cond)
        def _():
            kv_copy(jnp.maximum(from_slot, 0), jnp.maximum(to_slot, 0), number, target).start()

    def await_block(distance):
        slot = slot_of(distance)
        pltpu.make_async_copy(kv.at[slot], kv.at[slot], kv_recv.at[slot]).wait()

    def arrive(distance, numbers):
        @pl.when(me >= distance)
        def _():
            await_block(distance)
            for number in numbers:
                start_send(number)

    dec_copy = pltpu.make_async_remote_copy(
        src_ref=dec_own,
        dst_ref=dec_sib,
        send_sem=dec_sems.at[0],
        recv_sem=dec_sems.at[1],
        device_id=(sibling, head),
        device_id_type=MESH,
    )
    dec_copy.start()
    for number in (0, 1, 2):
        start_send(number)

    for load in loads[2:5]:
        load.wait()

    mine_at = pl.multiple_of(core * part, part)
    other_at = pl.multiple_of((1 - core) * part, part)

    def pair_copy(source, target, send, recv, j, seq_pos):
        return pltpu.make_async_remote_copy(
            src_ref=source.at[j],
            dst_ref=target.at[j],
            send_sem=send.at[j],
            recv_sem=recv.at[j],
            device_id=(seq_pos, head),
            device_id_type=MESH,
        )

    x_copy = lambda p: pair_copy(x_out, x_in, x_send, x_recv, p, sibling)
    t_copy = lambda p: pair_copy(t_out, t_in, t_send, t_recv, p, across)
    s_copy = lambda p: pair_copy(s_out, s_in, s_send, s_recv, p, onward)
    h_copy = lambda p: pair_copy(h_out, h_in, h_send, h_recv, p, sibling)

    def rows_at(p, base):
        return pl.ds(pl.multiple_of(base + (p % SPLIT) * chunk, chunk), chunk)

    @pl.when(group == 0)
    def _():
        s_in[...] = jnp.zeros(s_in.shape, BF)

    first = core == 0

    def of_pair(p):
        j = p // SPLIT
        h = j // 3
        d_own = dec_own[pl.ds(h, 1), :][:, 0:1]
        d_sib = dec_sib[pl.ds(h, 1), :][:, 0:1]
        u_own = upd[j, rows_at(p, mine_at), :]
        u_sib = x_in[p].astype(F32)
        return (
            jnp.where(first, d_own, d_sib),
            jnp.where(first, d_sib, d_own),
            jnp.where(first, u_own, u_sib),
            jnp.where(first, u_sib, u_own),
        )

    def sum_pair(p, carry):
        x_copy(p).wait_recv()
        _, decay1, u0, u1 = of_pair(p)
        both = decay1 * u0 + u1
        t_own[p] = both
        t_out[p] = both.astype(BF)
        t_copy(p).start()
        return carry

    per_head = 3 * SPLIT

    def sum_pairs(h):
        lax.fori_loop(h * per_head, (h + 1) * per_head, sum_pair, 0)

    def gradients(h):
        cols = slice(h * dim, (h + 1) * dim)
        key_norm = rms_rows(kv[own, 0].astype(F32)[:, cols])
        rate = jnp.broadcast_to(rates_ref[h : h + 1, :], (8, rows)).T[:, 0:1]
        err = -rate * kv[own, 1].astype(F32)[:, cols]
        key_pair = halves(key_norm)
        pre_gate = dot3(key_pair, halves(gate_ref[h]))
        pre_up = dot3(key_pair, halves(up_ref[h]))
        sig = jax.nn.sigmoid(pre_gate)
        active = pre_gate * sig
        back = dot3(halves(err), halves(downt[h]))
        key_t = halves(key_norm.T)
        grads = (
            dot3(key_t, halves(back * pre_up * (sig * (1.0 + pre_gate * (1.0 - sig))))),
            dot3(key_t, halves(back * active)),
            dot3(halves(err.T), halves(active * pre_up)),
        )
        for i, grad in enumerate(grads):
            size = jnp.sum(jnp.sum(grad * grad, axis=1, keepdims=True), axis=0, keepdims=True)
            upd[3 * h + i] = grad / (jnp.sqrt(size) + 1e-07)

    def orthogonalize(h):
        def sweep(turn, carry):
            for j in range(3 * h, 3 * h + 3):
                current = upd[j]
                low = current.astype(BF)
                gram = dot1(low, low, NT)
                gram_low = gram.astype(BF)
                poly = coef_b * gram + coef_c * dot1(gram_low, gram_low)
                upd[j] = coef_a * current + dot1(poly.astype(BF), low)
            return carry

        lax.fori_loop(0, NS_STEPS, sweep, 0)
        for p in range(h * per_head, (h + 1) * per_head):
            j = p // SPLIT
            if p % SPLIT == 0:
                upd[j] = -step_ref[0:1, h : h + 1] * upd[j]
            x_out[p] = upd[j, rows_at(p, other_at), :].astype(BF)
            x_copy(p).start()

    for h in range(heads):
        gradients(h)
        if h == 1:
            arrive(4, (3, 4, 5))
            pl.when(side == 1)(lambda: arrive(2, (8,)))
        if h == 0:
            dec_copy.wait()
            dec_chip[...] = dec_own[...] * dec_sib[...]
            dec_chip_copy = pltpu.make_async_remote_copy(
                src_ref=dec_chip,
                dst_ref=dec_across,
                send_sem=dec_sems.at[2],
                recv_sem=dec_sems.at[3],
                device_id=(across, head),
                device_id_type=MESH,
            )
            dec_chip_copy.start()
        else:
            sum_pairs(h - 1)
        orthogonalize(h)
    pl.when(side == 0)(lambda: arrive(2, (8,)))
    arrive(8, (6, 7))
    sum_pairs(heads - 1)
    dec_chip_copy.wait()

    near = side == 0

    def chain():
        def link(p, carry):
            h = p // SPLIT // 3
            t_copy(p).wait_recv()

            @pl.when(group > 0)
            def _():
                s_copy(p).wait_recv()

            c_own = dec_chip[pl.ds(h, 1), :][:, 0:1]
            c_far = dec_across[pl.ds(h, 1), :][:, 0:1]
            chip0 = jnp.where(near, c_own, c_far)
            chip1 = jnp.where(near, c_far, c_own)
            t_far = t_in[p].astype(F32)
            t_mine = t_own[p]
            t0 = jnp.where(near, t_mine, t_far)
            t1 = jnp.where(near, t_far, t_mine)
            enter = s_in[p].astype(F32)
            halfway = chip0 * enter + t0

            @pl.when(has_next)
            def _():
                s_out[p] = (chip1 * halfway + t1).astype(BF)
                s_copy(p).start()

            decay0, _, u0, _ = of_pair(p)
            before = jnp.where(near, enter, halfway)
            middle = decay0 * before + u0
            h_out[p] = jnp.where(first, middle, before).astype(BF)
            h_copy(p).start()
            state[p // SPLIT, rows_at(p, mine_at), :] = jnp.where(first, before, middle)
            return carry

        lax.fori_loop(0, pieces, link, 0)

    loads[5].wait()
    lane = lax.broadcasted_iota(jnp.int32, (rows, 256), 1)
    starts = [0, heads * dim - 256]
    for h in range(heads):
        begin = h * dim - starts[h]
        inside = (lane >= begin) & (lane < begin + dim)
        wide = q_ref[:, starts[h] : starts[h] + 256].astype(F32)
        qpad[h] = jnp.where(inside, wide, 0.0).astype(BF)
    acc[...] = jnp.zeros(acc.shape, F32)
    top[...] = jnp.full(top.shape, FAR, F32)
    total[...] = jnp.zeros(total.shape, F32)
    gap = lax.broadcasted_iota(jnp.int32, (rows, rows), 0) - lax.broadcasted_iota(
        jnp.int32, (rows, rows), 1
    )

    def attend(distance):
        slot = slot_of(distance)
        back = gap + distance * rows
        for h in range(heads):
            cols = slice(starts[h], starts[h] + 256)
            scores = dot1(qpad[h], kv[slot, 0, :, cols], NT) * scale
            if distance == 0:
                scores = jnp.where(back >= 0, scores, FAR)
            if distance == reach:
                scores = jnp.where(back < WINDOW, scores, FAR)
            old_top = top[h][:, 0:1]
            new_top = jnp.maximum(old_top, jnp.max(scores, axis=1, keepdims=True))
            weights = jnp.exp(scores - new_top)
            shrink = jnp.exp(old_top - new_top)
            total[h] = jnp.broadcast_to(
                total[h][:, 0:1] * shrink + jnp.sum(weights, axis=1, keepdims=True), (rows, 128)
            )
            acc[h] = acc[h] * shrink + dot1(weights.astype(BF), kv[slot, 1, :, cols])
            top[h] = jnp.broadcast_to(new_top, (rows, 128))

    def turn_of(distance):
        if distance % 2 == 1:
            await_block(distance)
        attend(distance)

    early = []
    for position, distance in enumerate((0, 1, 3, 2, 4, 8, 7, 5, 6)):
        if position % 2 == 0 and position // 2 + 1 < n_group:
            early.append(position // 2)
            pl.when(group == position // 2)(chain)
        if position == 6:
            arrive(6, (9,))
        pl.when(me >= distance)(functools.partial(turn_of, distance))

    for h in range(heads):
        cols = slice(h * dim, (h + 1) * dim)
        begin = h * dim - starts[h]
        attended = acc[h][:, begin : begin + dim] / total[h][:, 0:1]
        share_attn[h] = rms_rows(attended) * again_ref[...].reshape(1, -1)[:, cols]
        for i, piece in enumerate(halves(rms_rows(q_ref[...].astype(F32)[:, cols]))):
            query_pair[h, i] = piece

    pl.when(group > early[-1] if early else group >= 0)(chain)

    loads[6].wait()
    for p in range(pieces):
        h_copy(p).wait_recv()
        state[p // SPLIT, rows_at(p, other_at), :] = h_in[p].astype(F32)

    for h in range(heads):
        cols = slice(h * dim, (h + 1) * dim)
        query = (query_pair[h, 0], query_pair[h, 1])
        pre_gate = dot3(query, halves(gate_ref[h] + state[3 * h]))
        pre_up = dot3(query, halves(up_ref[h] + state[3 * h + 1]))
        hidden = pre_gate * jax.nn.sigmoid(pre_gate) * pre_up
        applied = dot3(halves(hidden), halves(downt[h] + state[3 * h + 2]), NT)
        mixed[h] = (
            rms_rows(applied) * tgain_ref[...].reshape(1, -1)[:, cols] + share_attn[h]
        ).astype(BF)

    share = rows // n_head

    def project(target):
        at = pl.multiple_of(target * share, share)
        result = dot1(mixed[0, pl.ds(at, share), :], proj_ref[0:dim, :])
        for h in range(1, heads):
            result = result + dot1(
                mixed[h, pl.ds(at, share), :], proj_ref[h * dim : (h + 1) * dim, :]
            )
        return result

    def p_copy(hop):
        return pltpu.make_async_remote_copy(
            src_ref=p_out.at[hop - 1],
            dst_ref=p_in.at[hop - 1],
            send_sem=p_send.at[hop - 1],
            recv_sem=p_recv.at[hop - 1],
            device_id=(me, lax.rem(head + hop, n_head)),
            device_id_type=MESH,
        )

    for hop in range(1, n_head):
        p_out[hop - 1] = project(lax.rem(head + hop, n_head)).astype(BF)
        p_copy(hop).start()
    result = project(head)
    for hop in range(1, n_head):
        p_copy(hop).wait_recv()
        result = result + p_in[hop - 1].astype(F32)
    out_ref[...] = result.astype(BF)

    for number, (cond, from_slot, to_slot, _, target) in enumerate(sends):

        @pl.when(cond)
        def _():
            kv_copy(
                jnp.maximum(from_slot, 0), jnp.maximum(to_slot, 0), number, target
            ).wait_send()

    for p in range(pieces):
        x_copy(p).wait_send()
        t_copy(p).wait_send()
        h_copy(p).wait_send()

        @pl.when(has_next)
        def _():
            s_copy(p).wait_send()

    for hop in range(1, n_head):
        p_copy(hop).wait_send()


def local(
    n_seq,
    n_head,
    query_rows,
    key_rows,
    value_rows,
    rates,
    fw_decay,
    fw_step,
    fast_gate,
    fast_up,
    fast_down,
    ttt_gain,
    attn_gain,
    out_proj,
):
    rows, cols = query_rows.shape
    heads, dim, fast = fast_gate.shape
    width = out_proj.shape[1]
    share = rows // n_head
    mats = 3 * heads
    slots = WINDOW // rows + GROUP
    dma = pltpu.SemaphoreType.DMA
    pieces = mats * SPLIT
    chunk = dim // 2 // SPLIT
    piece = pltpu.VMEM((pieces, chunk, fast), BF)
    moved = pl.BlockSpec(memory_space=pl.ANY)
    small = pl.BlockSpec(memory_space=pltpu.VMEM)
    return pl.pallas_call(
        functools.partial(kernel, n_seq, n_head),
        out_shape=jax.ShapeDtypeStruct((share, width), BF),
        in_specs=[moved] * 3 + [small] * 3 + [moved] * 3 + [small] * 2 + [moved],
        out_specs=pl.BlockSpec(memory_space=pltpu.VMEM),
        scratch_shapes=[
            pltpu.VMEM((rows, cols), BF),
            pltpu.VMEM((heads, dim, fast), F32),
            pltpu.VMEM((heads, dim, fast), F32),
            pltpu.VMEM((heads, dim, fast), F32),
            pltpu.VMEM((cols, width), BF),
            pltpu.VMEM((slots, 2, rows, cols), BF),
            pltpu.VMEM((8, 128), F32),
            pltpu.VMEM((8, 128), F32),
            pltpu.VMEM((8, 128), F32),
            pltpu.VMEM((8, 128), F32),
            pltpu.VMEM((mats, dim, fast), F32),
            piece,
            piece,
            pltpu.VMEM((pieces, chunk, fast), F32),
            piece,
            piece,
            piece,
            piece,
            piece,
            piece,
            pltpu.VMEM((mats, dim, fast), F32),
            pltpu.VMEM((heads, rows, 256), BF),
            pltpu.VMEM((heads, rows, 256), F32),
            pltpu.VMEM((heads, rows, 128), F32),
            pltpu.VMEM((heads, rows, 128), F32),
            pltpu.VMEM((heads, rows, dim), F32),
            pltpu.VMEM((heads, 2, rows, dim), BF),
            pltpu.VMEM((heads, rows, dim), BF),
            pltpu.VMEM((n_head - 1, share, width), BF),
            pltpu.VMEM((n_head - 1, share, width), BF),
            dma((7,)),
            dma((10,)),
            dma((slots,)),
            dma((4,)),
            dma((pieces,)),
            dma((pieces,)),
            dma((pieces,)),
            dma((pieces,)),
            dma((pieces,)),
            dma((pieces,)),
            dma((pieces,)),
            dma((pieces,)),
            dma((n_head - 1,)),
            dma((n_head - 1,)),
        ],
        compiler_params=pltpu.CompilerParams(
            collective_id=0, has_side_effects=True, vmem_limit_bytes=56 * 1024 * 1024
        ),
    )(
        query_rows,
        key_rows,
        value_rows,
        rates.T,
        fw_decay,
        fw_step.reshape(1, -1),
        fast_gate,
        fast_up,
        jnp.swapaxes(fast_down, 1, 2),
        ttt_gain,
        attn_gain,
        out_proj,
    )


def solution(mesh):
    in_specs = (
        P("seq", "head"),
        P("seq", "head"),
        P("seq", "head"),
        P("seq", "head"),
        P("seq", "head"),
        P("head"),
        P("head", None, None),
        P("head", None, None),
        P("head", None, None),
        P("head"),
        P("head"),
        P("head", None),
    )
    out_specs = P(("seq", "head"), None)
    body = functools.partial(local, mesh.shape["seq"], mesh.shape["head"])
    return jax.shard_map(body, mesh=mesh, in_specs=in_specs, out_specs=out_specs, check_vma=False)
```

```python
import functools
import math

import jax
import jax.numpy as jnp
from jax import lax
from jax.experimental import pallas as pl
from jax.experimental.pallas import tpu as pltpu
from jax.sharding import PartitionSpec as P

WINDOW = 2048
NS_STEPS = 5
GROUP = 4
SPLIT = 2
MESH = pl.DeviceIdType.MESH
BF = jnp.bfloat16
F32 = jnp.float32
coef_a = 3.4445
coef_b = -4.775
coef_c = 2.0315
FAR = -1e30

NN = (((1,), (0,)), ((), ()))
NT = (((1,), (1,)), ((), ()))


def dot1(left, right, dims=NN):
    return lax.dot_general(left, right, dims, preferred_element_type=F32)


def halves(value):
    high = value.astype(BF)
    return high, (value - high.astype(F32)).astype(BF)


def dot3(left, right, dims=NN):
    return dot1(left[0], right[0], dims) + (
        dot1(left[0], right[1], dims) + dot1(left[1], right[0], dims)
    )


def dot2(left, right):
    return dot1(left, right[0]) + dot1(left, right[1])


def rms_inverse(values):
    return lax.rsqrt(jnp.mean(values * values, axis=-1, keepdims=True) + 1e-06)


def rms_rows(values):
    return values * rms_inverse(values)


def kernel(
    n_seq,
    n_head,
    q_hbm,
    k_hbm,
    v_hbm,
    rates_ref,
    decay_ref,
    step_ref,
    gate_hbm,
    up_hbm,
    downt_hbm,
    tgain_ref,
    again_ref,
    proj_hbm,
    out_ref,
    q_ref,
    gate_ref,
    up_ref,
    downt,
    proj_ref,
    kv,
    dec_own,
    dec_sib,
    dec_chip,
    dec_across,
    upd,
    x_out,
    x_in,
    t_own,
    t_out,
    t_in,
    s_out,
    s_in,
    h_out,
    h_in,
    state,
    qpad,
    acc,
    top,
    total,
    share_attn,
    query_low,
    query_scale,
    mixed,
    p_out,
    p_in,
    load_sems,
    kv_send,
    kv_recv,
    dec_sems,
    x_send,
    x_recv,
    t_send,
    t_recv,
    s_send,
    s_recv,
    h_send,
    h_recv,
    p_send,
    p_recv,
):
    rows = q_ref.shape[0]
    heads, dim, _ = gate_ref.shape
    part = dim // 2
    chunk = part // SPLIT
    pieces = 3 * heads * SPLIT
    scale = 1.0 / math.sqrt(dim)
    reach = WINDOW // rows
    n_group = n_seq // GROUP
    me = lax.axis_index("seq")
    head = lax.axis_index("head")
    group = me // GROUP
    member = me % GROUP
    side = member // 2
    core = member % 2
    sibling = me + 1 - 2 * core
    across = me + 2 - 4 * side
    onward = me + GROUP
    own = reach + member

    loads = [
        pltpu.make_async_copy(source, target, load_sems.at[i])
        for i, (source, target) in enumerate(
            (
                (k_hbm, kv.at[own, 0]),
                (v_hbm, kv.at[own, 1]),
                (gate_hbm, gate_ref),
                (up_hbm, up_ref),
                (downt_hbm, downt),
                (q_hbm, q_ref),
                (proj_hbm, proj_ref),
            )
        )
    ]
    for load in loads:
        load.start()

    barrier = pltpu.get_barrier_semaphore()

    def greet(seq_pos, head_pos):
        pl.semaphore_signal(barrier, inc=1, device_id=(seq_pos, head_pos), device_id_type=MESH)

    greet(sibling, head)
    greet(across, head)
    expected = jnp.int32(2 + n_head - 1)
    for step in (GROUP, -GROUP):
        there = (me + step >= 0) & (me + step < n_seq)
        pl.when(there)(functools.partial(greet, me + step, head))
        expected = expected + there.astype(jnp.int32)
    for hop in range(1, n_head):
        greet(me, lax.rem(head + hop, n_head))

    dec_own[...] = jnp.zeros(dec_own.shape, F32)
    for h in range(heads):
        dec_own[h : h + 1, :] = jnp.broadcast_to(decay_ref[0:1, h : h + 1], (1, 128))
    loads[0].wait()
    loads[1].wait()
    pl.semaphore_wait(barrier, expected)

    def kv_copy(from_slot, to_slot, number, seq_pos):
        return pltpu.make_async_remote_copy(
            src_ref=kv.at[from_slot],
            dst_ref=kv.at[to_slot],
            send_sem=kv_send.at[number],
            recv_sem=kv_recv.at[to_slot],
            device_id=(seq_pos, head),
            device_id_type=MESH,
        )

    def slot_of(distance):
        return reach + member - distance

    has_next = group + 1 < n_group
    sends = [
        (has_next, own, own - GROUP, 0, onward),
        (side == 0, own, own, 1, across),
        (core == 0, own, own, 2, sibling),
        (has_next & (me >= 4), slot_of(4), slot_of(8), 3, onward),
        (me >= 4, slot_of(4), slot_of(4), 4, across),
        (me >= 4, slot_of(4), slot_of(4), 5, sibling),
        (has_next & (me >= 4) & (side == 0), slot_of(2), slot_of(6), 6, onward),
        ((me >= 8) & (core == 1), slot_of(8), slot_of(8), 7, sibling),
        (me >= 2, slot_of(2), slot_of(2), 8, sibling),
        (me >= 6, slot_of(6), slot_of(6), 9, sibling),
    ]

    def start_send(number):
        cond, from_slot, to_slot, _, target = sends[number]

        @pl.when(cond)
        def _():
            kv_copy(jnp.maximum(from_slot, 0), jnp.maximum(to_slot, 0), number, target).start()

    def await_block(distance):
        slot = slot_of(distance)
        pltpu.make_async_copy(kv.at[slot], kv.at[slot], kv_recv.at[slot]).wait()

    def arrive(distance, numbers):
        @pl.when(me >= distance)
        def _():
            await_block(distance)
            for number in numbers:
                start_send(number)

    dec_copy = pltpu.make_async_remote_copy(
        src_ref=dec_own,
        dst_ref=dec_sib,
        send_sem=dec_sems.at[0],
        recv_sem=dec_sems.at[1],
        device_id=(sibling, head),
        device_id_type=MESH,
    )
    dec_copy.start()
    for number in (0, 1, 2):
        start_send(number)

    for load in loads[2:5]:
        load.wait()

    mine_at = pl.multiple_of(core * part, part)
    other_at = pl.multiple_of((1 - core) * part, part)

    def pair_copy(source, target, send, recv, j, seq_pos):
        return pltpu.make_async_remote_copy(
            src_ref=source.at[j],
            dst_ref=target.at[j],
            send_sem=send.at[j],
            recv_sem=recv.at[j],
            device_id=(seq_pos, head),
            device_id_type=MESH,
        )

    x_copy = lambda p: pair_copy(x_out, x_in, x_send, x_recv, p, sibling)
    t_copy = lambda p: pair_copy(t_out, t_in, t_send, t_recv, p, across)
    s_copy = lambda p: pair_copy(s_out, s_in, s_send, s_recv, p, onward)
    h_copy = lambda p: pair_copy(h_out, h_in, h_send, h_recv, p, sibling)

    def rows_at(p, base):
        return pl.ds(pl.multiple_of(base + (p % SPLIT) * chunk, chunk), chunk)

    @pl.when(group == 0)
    def _():
        s_in[...] = jnp.zeros(s_in.shape, BF)

    first = core == 0

    def of_pair(p):
        j = p // SPLIT
        h = j // 3
        d_own = dec_own[pl.ds(h, 1), :][:, 0:1]
        d_sib = dec_sib[pl.ds(h, 1), :][:, 0:1]
        u_own = upd[j, rows_at(p, mine_at), :]
        u_sib = x_in[p].astype(F32)
        return (
            jnp.where(first, d_own, d_sib),
            jnp.where(first, d_sib, d_own),
            jnp.where(first, u_own, u_sib),
            jnp.where(first, u_sib, u_own),
        )

    def sum_pair(p, carry):
        x_copy(p).wait_recv()
        _, decay1, u0, u1 = of_pair(p)
        both = decay1 * u0 + u1
        t_own[p] = both
        t_out[p] = both.astype(BF)
        t_copy(p).start()
        return carry

    per_head = 3 * SPLIT

    def sum_pairs(h):
        lax.fori_loop(h * per_head, (h + 1) * per_head, sum_pair, 0)

    def gradients(h):
        cols = slice(h * dim, (h + 1) * dim)
        key = kv[own, 0].astype(F32)[:, cols]
        value = kv[own, 1].astype(F32)[:, cols]
        key_scale = rms_inverse(key)
        rate = -jnp.broadcast_to(rates_ref[h : h + 1, :], (8, rows)).T[:, 0:1]
        key_low = key.astype(BF)
        pre_gate = key_scale * dot2(key_low, halves(gate_ref[h]))
        pre_up = key_scale * dot2(key_low, halves(up_ref[h]))
        sig = jax.nn.sigmoid(pre_gate)
        active = pre_gate * sig
        back = (rate * key_scale) * dot2(value.astype(BF), halves(downt[h]))
        key_t = key.T.astype(BF)
        grads = (
            dot2(key_t, halves(back * pre_up * (sig * (1.0 + pre_gate * (1.0 - sig))))),
            dot2(key_t, halves(back * active)),
            dot2(value.T.astype(BF), halves(rate * active * pre_up)),
        )
        for i, grad in enumerate(grads):
            size = jnp.sum(jnp.sum(grad * grad, axis=1, keepdims=True), axis=0, keepdims=True)
            upd[3 * h + i] = grad / (jnp.sqrt(size) + 1e-07)

    def orthogonalize(h):
        def sweep(turn, carry):
            for j in range(3 * h, 3 * h + 3):
                current = upd[j]
                low = current.astype(BF)
                gram = dot1(low, low, NT)
                gram_low = gram.astype(BF)
                poly = coef_b * gram + coef_c * dot1(gram_low, gram_low)
                upd[j] = coef_a * current + dot1(poly.astype(BF), low)
            return carry

        lax.fori_loop(0, NS_STEPS, sweep, 0)
        for p in range(h * per_head, (h + 1) * per_head):
            j = p // SPLIT
            if p % SPLIT == 0:
                upd[j] = -step_ref[0:1, h : h + 1] * upd[j]
            x_out[p] = upd[j, rows_at(p, other_at), :].astype(BF)
            x_copy(p).start()

    for h in range(heads):
        gradients(h)
        if h == 1:
            pl.when(side == 1)(lambda: arrive(2, (8,)))
        if h == 0:
            dec_copy.wait()
            dec_chip[...] = dec_own[...] * dec_sib[...]
            dec_chip_copy = pltpu.make_async_remote_copy(
                src_ref=dec_chip,
                dst_ref=dec_across,
                send_sem=dec_sems.at[2],
                recv_sem=dec_sems.at[3],
                device_id=(across, head),
                device_id_type=MESH,
            )
            dec_chip_copy.start()
        else:
            sum_pairs(h - 1)
        orthogonalize(h)
        if h == 0:
            arrive(4, (3, 4, 5))
    pl.when(side == 0)(lambda: arrive(2, (6, 8)))
    arrive(8, (7,))
    sum_pairs(heads - 1)
    dec_chip_copy.wait()

    near = side == 0

    def chain():
        def link(p, carry):
            h = p // SPLIT // 3
            t_copy(p).wait_recv()

            @pl.when(group > 0)
            def _():
                s_copy(p).wait_recv()

            c_own = dec_chip[pl.ds(h, 1), :][:, 0:1]
            c_far = dec_across[pl.ds(h, 1), :][:, 0:1]
            chip0 = jnp.where(near, c_own, c_far)
            chip1 = jnp.where(near, c_far, c_own)
            t_far = t_in[p].astype(F32)
            t_mine = t_own[p]
            t0 = jnp.where(near, t_mine, t_far)
            t1 = jnp.where(near, t_far, t_mine)
            enter = s_in[p].astype(F32)
            halfway = chip0 * enter + t0

            @pl.when(has_next)
            def _():
                s_out[p] = (chip1 * halfway + t1).astype(BF)
                s_copy(p).start()

            decay0, _, u0, _ = of_pair(p)
            before = jnp.where(near, enter, halfway)
            middle = decay0 * before + u0
            h_out[p] = jnp.where(first, middle, before).astype(BF)
            h_copy(p).start()
            state[p // SPLIT, rows_at(p, mine_at), :] = jnp.where(first, before, middle)
            return carry

        lax.fori_loop(0, pieces, link, 0)

    loads[5].wait()
    lane = lax.broadcasted_iota(jnp.int32, (rows, 256), 1)
    starts = [0, heads * dim - 256]
    for h in range(heads):
        begin = h * dim - starts[h]
        inside = (lane >= begin) & (lane < begin + dim)
        wide = q_ref[:, starts[h] : starts[h] + 256].astype(F32)
        qpad[h] = jnp.where(inside, wide, 0.0).astype(BF)
    acc[...] = jnp.zeros(acc.shape, F32)
    top[...] = jnp.full(top.shape, FAR, F32)
    total[...] = jnp.zeros(total.shape, F32)
    gap = lax.broadcasted_iota(jnp.int32, (rows, rows), 0) - lax.broadcasted_iota(
        jnp.int32, (rows, rows), 1
    )

    def attend(distance):
        slot = slot_of(distance)
        back = gap + distance * rows
        for h in range(heads):
            cols = slice(starts[h], starts[h] + 256)
            scores = dot1(qpad[h], kv[slot, 0, :, cols], NT) * scale
            if distance == 0:
                scores = jnp.where(back >= 0, scores, FAR)
            if distance == reach:
                scores = jnp.where(back < WINDOW, scores, FAR)
            old_top = top[h][:, 0:1]
            new_top = jnp.maximum(old_top, jnp.max(scores, axis=1, keepdims=True))
            weights = jnp.exp(scores - new_top)
            shrink = jnp.exp(old_top - new_top)
            total[h] = jnp.broadcast_to(
                total[h][:, 0:1] * shrink + jnp.sum(weights, axis=1, keepdims=True), (rows, 128)
            )
            acc[h] = acc[h] * shrink + dot1(weights.astype(BF), kv[slot, 1, :, cols])
            top[h] = jnp.broadcast_to(new_top, (rows, 128))

    def turn_of(distance):
        if distance % 2 == 1:
            await_block(distance)
        attend(distance)

    early = []
    for position, distance in enumerate((0, 1, 3, 2, 4, 8, 7, 5, 6)):
        if position % 2 == 0 and position // 2 + 1 < n_group:
            early.append(position // 2)
            pl.when(group == position // 2)(chain)
        if position == 6:
            arrive(6, (9,))
        pl.when(me >= distance)(functools.partial(turn_of, distance))

    for h in range(heads):
        cols = slice(h * dim, (h + 1) * dim)
        begin = h * dim - starts[h]
        attended = acc[h][:, begin : begin + dim] / total[h][:, 0:1]
        share_attn[h] = rms_rows(attended) * again_ref[...].reshape(1, -1)[:, cols]
        query = q_ref[...].astype(F32)[:, cols]
        query_low[h] = query.astype(BF)
        query_scale[h] = jnp.broadcast_to(rms_inverse(query), (rows, 128))

    pl.when(group > early[-1] if early else group >= 0)(chain)

    loads[6].wait()
    for p in range(pieces):
        h_copy(p).wait_recv()
        state[p // SPLIT, rows_at(p, other_at), :] = h_in[p].astype(F32)

    for h in range(heads):
        cols = slice(h * dim, (h + 1) * dim)
        query = query_low[h]
        scale_q = query_scale[h][:, 0:1]
        pre_gate = scale_q * dot2(query, halves(gate_ref[h] + state[3 * h]))
        pre_up = scale_q * dot2(query, halves(up_ref[h] + state[3 * h + 1]))
        hidden = pre_gate * jax.nn.sigmoid(pre_gate) * pre_up
        applied = dot3(halves(hidden), halves(downt[h] + state[3 * h + 2]), NT)
        mixed[h] = (
            rms_rows(applied) * tgain_ref[...].reshape(1, -1)[:, cols] + share_attn[h]
        ).astype(BF)

    share = rows // n_head

    def project(target):
        at = pl.multiple_of(target * share, share)
        result = dot1(mixed[0, pl.ds(at, share), :], proj_ref[0:dim, :])
        for h in range(1, heads):
            result = result + dot1(
                mixed[h, pl.ds(at, share), :], proj_ref[h * dim : (h + 1) * dim, :]
            )
        return result

    def p_copy(hop):
        return pltpu.make_async_remote_copy(
            src_ref=p_out.at[hop - 1],
            dst_ref=p_in.at[hop - 1],
            send_sem=p_send.at[hop - 1],
            recv_sem=p_recv.at[hop - 1],
            device_id=(me, lax.rem(head + hop, n_head)),
            device_id_type=MESH,
        )

    for hop in range(1, n_head):
        p_out[hop - 1] = project(lax.rem(head + hop, n_head)).astype(BF)
        p_copy(hop).start()
    result = project(head)
    for hop in range(1, n_head):
        p_copy(hop).wait_recv()
        result = result + p_in[hop - 1].astype(F32)
    out_ref[...] = result.astype(BF)

    for number, (cond, from_slot, to_slot, _, target) in enumerate(sends):

        @pl.when(cond)
        def _():
            kv_copy(
                jnp.maximum(from_slot, 0), jnp.maximum(to_slot, 0), number, target
            ).wait_send()

    for p in range(pieces):
        x_copy(p).wait_send()
        t_copy(p).wait_send()
        h_copy(p).wait_send()

        @pl.when(has_next)
        def _():
            s_copy(p).wait_send()

    for hop in range(1, n_head):
        p_copy(hop).wait_send()


def local(
    n_seq,
    n_head,
    query_rows,
    key_rows,
    value_rows,
    rates,
    fw_decay,
    fw_step,
    fast_gate,
    fast_up,
    fast_down,
    ttt_gain,
    attn_gain,
    out_proj,
):
    rows, cols = query_rows.shape
    heads, dim, fast = fast_gate.shape
    width = out_proj.shape[1]
    share = rows // n_head
    mats = 3 * heads
    slots = WINDOW // rows + GROUP
    dma = pltpu.SemaphoreType.DMA
    pieces = mats * SPLIT
    chunk = dim // 2 // SPLIT
    piece = pltpu.VMEM((pieces, chunk, fast), BF)
    moved = pl.BlockSpec(memory_space=pl.ANY)
    small = pl.BlockSpec(memory_space=pltpu.VMEM)
    return pl.pallas_call(
        functools.partial(kernel, n_seq, n_head),
        out_shape=jax.ShapeDtypeStruct((share, width), BF),
        in_specs=[moved] * 3 + [small] * 3 + [moved] * 3 + [small] * 2 + [moved],
        out_specs=pl.BlockSpec(memory_space=pltpu.VMEM),
        scratch_shapes=[
            pltpu.VMEM((rows, cols), BF),
            pltpu.VMEM((heads, dim, fast), F32),
            pltpu.VMEM((heads, dim, fast), F32),
            pltpu.VMEM((heads, dim, fast), F32),
            pltpu.VMEM((cols, width), BF),
            pltpu.VMEM((slots, 2, rows, cols), BF),
            pltpu.VMEM((8, 128), F32),
            pltpu.VMEM((8, 128), F32),
            pltpu.VMEM((8, 128), F32),
            pltpu.VMEM((8, 128), F32),
            pltpu.VMEM((mats, dim, fast), F32),
            piece,
            piece,
            pltpu.VMEM((pieces, chunk, fast), F32),
            piece,
            piece,
            piece,
            piece,
            piece,
            piece,
            pltpu.VMEM((mats, dim, fast), F32),
            pltpu.VMEM((heads, rows, 256), BF),
            pltpu.VMEM((heads, rows, 256), F32),
            pltpu.VMEM((heads, rows, 128), F32),
            pltpu.VMEM((heads, rows, 128), F32),
            pltpu.VMEM((heads, rows, dim), F32),
            pltpu.VMEM((heads, rows, dim), BF),
            pltpu.VMEM((heads, rows, 128), F32),
            pltpu.VMEM((heads, rows, dim), BF),
            pltpu.VMEM((n_head - 1, share, width), BF),
            pltpu.VMEM((n_head - 1, share, width), BF),
            dma((7,)),
            dma((10,)),
            dma((slots,)),
            dma((4,)),
            dma((pieces,)),
            dma((pieces,)),
            dma((pieces,)),
            dma((pieces,)),
            dma((pieces,)),
            dma((pieces,)),
            dma((pieces,)),
            dma((pieces,)),
            dma((n_head - 1,)),
            dma((n_head - 1,)),
        ],
        compiler_params=pltpu.CompilerParams(
            collective_id=0, has_side_effects=True, vmem_limit_bytes=56 * 1024 * 1024
        ),
    )(
        query_rows,
        key_rows,
        value_rows,
        rates.T,
        fw_decay,
        fw_step.reshape(1, -1),
        fast_gate,
        fast_up,
        jnp.swapaxes(fast_down, 1, 2),
        ttt_gain,
        attn_gain,
        out_proj,
    )


def solution(mesh):
    in_specs = (
        P("seq", "head"),
        P("seq", "head"),
        P("seq", "head"),
        P("seq", "head"),
        P("seq", "head"),
        P("head"),
        P("head", None, None),
        P("head", None, None),
        P("head", None, None),
        P("head"),
        P("head"),
        P("head", None),
    )
    out_specs = P(("seq", "head"), None)
    body = functools.partial(local, mesh.shape["seq"], mesh.shape["head"])
    return jax.shard_map(body, mesh=mesh, in_specs=in_specs, out_specs=out_specs, check_vma=False)
```

```python
import functools
import math

import jax
import jax.numpy as jnp
from jax import lax
from jax.experimental import pallas as pl
from jax.experimental.pallas import tpu as pltpu
from jax.sharding import PartitionSpec as P

WINDOW = 2048
NS_STEPS = 5
GROUP = 4
SPLIT = 2
MESH = pl.DeviceIdType.MESH
BF = jnp.bfloat16
F32 = jnp.float32
coef_a = 3.4445
coef_b = -4.775
coef_c = 2.0315
FAR = -1e30

NN = (((1,), (0,)), ((), ()))
NT = (((1,), (1,)), ((), ()))


def dot1(left, right, dims=NN):
    return lax.dot_general(left, right, dims, preferred_element_type=F32)


def halves(value):
    high = value.astype(BF)
    return high, (value - high.astype(F32)).astype(BF)


def dot3(left, right, dims=NN):
    return dot1(left[0], right[0], dims) + (
        dot1(left[0], right[1], dims) + dot1(left[1], right[0], dims)
    )


def dot2(left, right):
    return dot1(left, right[0]) + dot1(left, right[1])


def rms_inverse(values):
    return lax.rsqrt(jnp.mean(values * values, axis=-1, keepdims=True) + 1e-06)


def rms_rows(values):
    return values * rms_inverse(values)


def kernel(
    n_seq,
    n_head,
    q_hbm,
    k_hbm,
    v_hbm,
    rates_ref,
    decay_ref,
    step_ref,
    gate_hbm,
    up_hbm,
    downt_hbm,
    tgain_ref,
    again_ref,
    proj_hbm,
    out_ref,
    q_ref,
    gate_ref,
    up_ref,
    downt,
    proj_ref,
    kv,
    dec_own,
    dec_sib,
    dec_chip,
    dec_across,
    upd,
    x_out,
    x_in,
    t_own,
    t_out,
    t_in,
    s_out,
    s_in,
    h_out,
    h_in,
    state,
    qpad,
    acc,
    top,
    total,
    share_attn,
    query_low,
    query_scale,
    mixed,
    p_out,
    p_in,
    load_sems,
    kv_send,
    kv_recv,
    dec_sems,
    x_send,
    x_recv,
    t_send,
    t_recv,
    s_send,
    s_recv,
    h_send,
    h_recv,
    p_send,
    p_recv,
):
    rows = q_ref.shape[0]
    heads, dim, _ = gate_ref.shape
    part = dim // 2
    chunk = part // SPLIT
    pieces = 3 * heads * SPLIT
    scale = 1.0 / math.sqrt(dim)
    reach = WINDOW // rows
    n_group = n_seq // GROUP
    me = lax.axis_index("seq")
    head = lax.axis_index("head")
    group = me // GROUP
    member = me % GROUP
    side = member // 2
    core = member % 2
    sibling = me + 1 - 2 * core
    across = me + 2 - 4 * side
    onward = me + GROUP
    own = reach + member

    loads = [
        pltpu.make_async_copy(source, target, load_sems.at[i])
        for i, (source, target) in enumerate(
            (
                (k_hbm, kv.at[own, 0]),
                (v_hbm, kv.at[own, 1]),
                (gate_hbm, gate_ref),
                (up_hbm, up_ref),
                (downt_hbm, downt),
                (q_hbm, q_ref),
                (proj_hbm, proj_ref),
            )
        )
    ]
    for load in loads:
        load.start()

    barrier = pltpu.get_barrier_semaphore()

    def greet(seq_pos, head_pos):
        pl.semaphore_signal(barrier, inc=1, device_id=(seq_pos, head_pos), device_id_type=MESH)

    greet(sibling, head)
    greet(across, head)
    expected = jnp.int32(2 + n_head - 1)
    for step in (GROUP, -GROUP):
        there = (me + step >= 0) & (me + step < n_seq)
        pl.when(there)(functools.partial(greet, me + step, head))
        expected = expected + there.astype(jnp.int32)
    for hop in range(1, n_head):
        greet(me, lax.rem(head + hop, n_head))

    dec_own[...] = jnp.zeros(dec_own.shape, F32)
    for h in range(heads):
        dec_own[h : h + 1, :] = jnp.broadcast_to(decay_ref[0:1, h : h + 1], (1, 128))
    loads[0].wait()
    loads[1].wait()
    pl.semaphore_wait(barrier, expected)

    def kv_copy(from_slot, to_slot, number, seq_pos):
        return pltpu.make_async_remote_copy(
            src_ref=kv.at[from_slot],
            dst_ref=kv.at[to_slot],
            send_sem=kv_send.at[number],
            recv_sem=kv_recv.at[to_slot],
            device_id=(seq_pos, head),
            device_id_type=MESH,
        )

    def slot_of(distance):
        return reach + member - distance

    has_next = group + 1 < n_group
    sends = [
        (has_next, own, own - GROUP, 0, onward),
        (side == 0, own, own, 1, across),
        (core == 0, own, own, 2, sibling),
        (has_next & (me >= 4), slot_of(4), slot_of(8), 3, onward),
        (me >= 4, slot_of(4), slot_of(4), 4, across),
        (me >= 4, slot_of(4), slot_of(4), 5, sibling),
        (has_next & (me >= 4) & (side == 0), slot_of(2), slot_of(6), 6, onward),
        ((me >= 8) & (core == 1), slot_of(8), slot_of(8), 7, sibling),
        (me >= 2, slot_of(2), slot_of(2), 8, sibling),
        (me >= 6, slot_of(6), slot_of(6), 9, sibling),
    ]

    def start_send(number):
        cond, from_slot, to_slot, _, target = sends[number]

        @pl.when(cond)
        def _():
            kv_copy(jnp.maximum(from_slot, 0), jnp.maximum(to_slot, 0), number, target).start()

    def await_block(distance):
        slot = slot_of(distance)
        pltpu.make_async_copy(kv.at[slot], kv.at[slot], kv_recv.at[slot]).wait()

    def arrive(distance, numbers):
        @pl.when(me >= distance)
        def _():
            await_block(distance)
            for number in numbers:
                start_send(number)

    dec_copy = pltpu.make_async_remote_copy(
        src_ref=dec_own,
        dst_ref=dec_sib,
        send_sem=dec_sems.at[0],
        recv_sem=dec_sems.at[1],
        device_id=(sibling, head),
        device_id_type=MESH,
    )
    dec_copy.start()
    for number in (0, 1, 2):
        start_send(number)

    for load in loads[2:5]:
        load.wait()

    mine_at = pl.multiple_of(core * part, part)
    other_at = pl.multiple_of((1 - core) * part, part)

    def pair_copy(source, target, send, recv, j, seq_pos):
        return pltpu.make_async_remote_copy(
            src_ref=source.at[j],
            dst_ref=target.at[j],
            send_sem=send.at[j],
            recv_sem=recv.at[j],
            device_id=(seq_pos, head),
            device_id_type=MESH,
        )

    x_copy = lambda p: pair_copy(x_out, x_in, x_send, x_recv, p, sibling)
    t_copy = lambda p: pair_copy(t_out, t_in, t_send, t_recv, p, across)
    s_copy = lambda p: pair_copy(s_out, s_in, s_send, s_recv, p, onward)
    h_copy = lambda p: pair_copy(h_out, h_in, h_send, h_recv, p, sibling)

    def rows_at(p, base):
        return pl.ds(pl.multiple_of(base + (p % SPLIT) * chunk, chunk), chunk)

    @pl.when(group == 0)
    def _():
        s_in[...] = jnp.zeros(s_in.shape, BF)

    first = core == 0

    def of_pair(p):
        j = p // SPLIT
        h = j // 3
        d_own = dec_own[pl.ds(h, 1), :][:, 0:1]
        d_sib = dec_sib[pl.ds(h, 1), :][:, 0:1]
        u_own = upd[j, rows_at(p, mine_at), :]
        u_sib = x_in[p].astype(F32)
        return (
            jnp.where(first, d_own, d_sib),
            jnp.where(first, d_sib, d_own),
            jnp.where(first, u_own, u_sib),
            jnp.where(first, u_sib, u_own),
        )

    def sum_pair(p, carry):
        x_copy(p).wait_recv()
        _, decay1, u0, u1 = of_pair(p)
        both = decay1 * u0 + u1
        t_own[p] = both
        t_out[p] = both.astype(BF)
        t_copy(p).start()
        return carry

    per_head = 3 * SPLIT

    def sum_pairs(h):
        lax.fori_loop(h * per_head, (h + 1) * per_head, sum_pair, 0)

    def gradients(h):
        cols = slice(h * dim, (h + 1) * dim)
        key = kv[own, 0].astype(F32)[:, cols]
        value = kv[own, 1].astype(F32)[:, cols]
        key_scale = rms_inverse(key)
        rate = -jnp.broadcast_to(rates_ref[h : h + 1, :], (8, rows)).T[:, 0:1]
        key_low = key.astype(BF)
        pre_gate = key_scale * dot2(key_low, halves(gate_ref[h]))
        pre_up = key_scale * dot2(key_low, halves(up_ref[h]))
        sig = jax.nn.sigmoid(pre_gate)
        active = pre_gate * sig
        back = (rate * key_scale) * dot2(value.astype(BF), halves(downt[h]))
        key_t = key.T.astype(BF)
        grads = (
            dot2(key_t, halves(back * pre_up * (sig * (1.0 + pre_gate * (1.0 - sig))))),
            dot2(key_t, halves(back * active)),
            dot2(value.T.astype(BF), halves(rate * active * pre_up)),
        )
        for i, grad in enumerate(grads):
            size = jnp.sum(jnp.sum(grad * grad, axis=1, keepdims=True), axis=0, keepdims=True)
            upd[3 * h + i] = grad / (jnp.sqrt(size) + 1e-07)

    def orthogonalize(h):
        def sweep(turn, carry):
            for j in range(3 * h, 3 * h + 3):
                current = upd[j]
                low = current.astype(BF)
                gram = dot1(low, low, NT)
                gram_low = gram.astype(BF)
                poly = coef_b * gram + coef_c * dot1(gram_low, gram_low)
                upd[j] = coef_a * current + dot1(poly.astype(BF), low)
            return carry

        lax.fori_loop(0, NS_STEPS, sweep, 0)
        for p in range(h * per_head, (h + 1) * per_head):
            j = p // SPLIT
            if p % SPLIT == 0:
                upd[j] = -step_ref[0:1, h : h + 1] * upd[j]
            x_out[p] = upd[j, rows_at(p, other_at), :].astype(BF)
            x_copy(p).start()

    near = side == 0

    def chain(head_id):
        def link(p, carry):
            h = p // SPLIT // 3
            t_copy(p).wait_recv()

            @pl.when(group > 0)
            def _():
                s_copy(p).wait_recv()

            c_own = dec_chip[pl.ds(h, 1), :][:, 0:1]
            c_far = dec_across[pl.ds(h, 1), :][:, 0:1]
            chip0 = jnp.where(near, c_own, c_far)
            chip1 = jnp.where(near, c_far, c_own)
            t_far = t_in[p].astype(F32)
            t_mine = t_own[p]
            t0 = jnp.where(near, t_mine, t_far)
            t1 = jnp.where(near, t_far, t_mine)
            enter = s_in[p].astype(F32)
            halfway = chip0 * enter + t0

            @pl.when(has_next)
            def _():
                s_out[p] = (chip1 * halfway + t1).astype(BF)
                s_copy(p).start()

            decay0, _, u0, _ = of_pair(p)
            before = jnp.where(near, enter, halfway)
            middle = decay0 * before + u0
            h_out[p] = jnp.where(first, middle, before).astype(BF)
            h_copy(p).start()
            state[p // SPLIT, rows_at(p, mine_at), :] = jnp.where(first, before, middle)
            return carry

        lax.fori_loop(head_id * per_head, (head_id + 1) * per_head, link, 0)

    for h in range(heads):
        gradients(h)
        if h == 1:
            pl.when(side == 1)(lambda: arrive(2, (8,)))
        if h == 0:
            dec_copy.wait()
            dec_chip[...] = dec_own[...] * dec_sib[...]
            dec_chip_copy = pltpu.make_async_remote_copy(
                src_ref=dec_chip,
                dst_ref=dec_across,
                send_sem=dec_sems.at[2],
                recv_sem=dec_sems.at[3],
                device_id=(across, head),
                device_id_type=MESH,
            )
            dec_chip_copy.start()
        else:
            if h == 1:
                dec_chip_copy.wait()
            sum_pairs(h - 1)
        orthogonalize(h)
        if h == 0:
            arrive(4, (3, 4, 5))
    pl.when(group == 0)(lambda: chain(0))
    sum_pairs(heads - 1)
    pl.when(side == 0)(lambda: arrive(2, (6, 8)))
    arrive(8, (7,))

    loads[5].wait()
    lane = lax.broadcasted_iota(jnp.int32, (rows, 256), 1)
    starts = [0, heads * dim - 256]
    for h in range(heads):
        begin = h * dim - starts[h]
        inside = (lane >= begin) & (lane < begin + dim)
        wide = q_ref[:, starts[h] : starts[h] + 256].astype(F32)
        qpad[h] = jnp.where(inside, wide, 0.0).astype(BF)
    acc[...] = jnp.zeros(acc.shape, F32)
    top[...] = jnp.full(top.shape, FAR, F32)
    total[...] = jnp.zeros(total.shape, F32)
    gap = lax.broadcasted_iota(jnp.int32, (rows, rows), 0) - lax.broadcasted_iota(
        jnp.int32, (rows, rows), 1
    )

    def attend(distance):
        slot = slot_of(distance)
        back = gap + distance * rows
        for h in range(heads):
            cols = slice(starts[h], starts[h] + 256)
            scores = dot1(qpad[h], kv[slot, 0, :, cols], NT) * scale
            if distance == 0:
                scores = jnp.where(back >= 0, scores, FAR)
            if distance == reach:
                scores = jnp.where(back < WINDOW, scores, FAR)
            old_top = top[h][:, 0:1]
            new_top = jnp.maximum(old_top, jnp.max(scores, axis=1, keepdims=True))
            weights = jnp.exp(scores - new_top)
            shrink = jnp.exp(old_top - new_top)
            total[h] = jnp.broadcast_to(
                total[h][:, 0:1] * shrink + jnp.sum(weights, axis=1, keepdims=True), (rows, 128)
            )
            acc[h] = acc[h] * shrink + dot1(weights.astype(BF), kv[slot, 1, :, cols])
            top[h] = jnp.broadcast_to(new_top, (rows, 128))

    def turn_of(distance):
        if distance % 2 == 1:
            await_block(distance)
        attend(distance)

    last_at = {0: 2, 1: 6}

    def rest():
        for h in range(1, heads):
            chain(h)

    for position, distance in enumerate((0, 1, 3, 2, 4, 8, 7, 5, 6)):
        if position == 6:
            arrive(6, (9,))
        if position in (2, 4, 6, 8) and position // 2 < n_group:
            pl.when(group == position // 2)(lambda: chain(0))
        for g, at in last_at.items():
            if at == position:
                pl.when(group == g)(rest)
        pl.when(me >= distance)(functools.partial(turn_of, distance))

    for h in range(heads):
        cols = slice(h * dim, (h + 1) * dim)
        begin = h * dim - starts[h]
        attended = acc[h][:, begin : begin + dim] / total[h][:, 0:1]
        share_attn[h] = rms_rows(attended) * again_ref[...].reshape(1, -1)[:, cols]
        query = q_ref[...].astype(F32)[:, cols]
        query_low[h] = query.astype(BF)
        query_scale[h] = jnp.broadcast_to(rms_inverse(query), (rows, 128))

    pl.when(group > 4)(lambda: chain(0))

    pl.when((group > 1) & has_next)(rest)
    loads[6].wait()
    for h in range(heads):
        if h == 1:
            pl.when((group > 1) & (group + 1 == n_group))(rest)
        for p in range(h * per_head, (h + 1) * per_head):
            h_copy(p).wait_recv()
            state[p // SPLIT, rows_at(p, other_at), :] = h_in[p].astype(F32)
        cols = slice(h * dim, (h + 1) * dim)
        query = query_low[h]
        scale_q = query_scale[h][:, 0:1]
        pre_gate = scale_q * dot2(query, halves(gate_ref[h] + state[3 * h]))
        pre_up = scale_q * dot2(query, halves(up_ref[h] + state[3 * h + 1]))
        hidden = pre_gate * jax.nn.sigmoid(pre_gate) * pre_up
        applied = dot3(halves(hidden), halves(downt[h] + state[3 * h + 2]), NT)
        mixed[h] = (
            rms_rows(applied) * tgain_ref[...].reshape(1, -1)[:, cols] + share_attn[h]
        ).astype(BF)

    share = rows // n_head

    def project(target):
        at = pl.multiple_of(target * share, share)
        result = dot1(mixed[0, pl.ds(at, share), :], proj_ref[0:dim, :])
        for h in range(1, heads):
            result = result + dot1(
                mixed[h, pl.ds(at, share), :], proj_ref[h * dim : (h + 1) * dim, :]
            )
        return result

    def p_copy(hop):
        return pltpu.make_async_remote_copy(
            src_ref=p_out.at[hop - 1],
            dst_ref=p_in.at[hop - 1],
            send_sem=p_send.at[hop - 1],
            recv_sem=p_recv.at[hop - 1],
            device_id=(me, lax.rem(head + hop, n_head)),
            device_id_type=MESH,
        )

    for hop in range(1, n_head):
        p_out[hop - 1] = project(lax.rem(head + hop, n_head)).astype(BF)
        p_copy(hop).start()
    result = project(head)
    for hop in range(1, n_head):
        p_copy(hop).wait_recv()
        result = result + p_in[hop - 1].astype(F32)
    out_ref[...] = result.astype(BF)

    for number, (cond, from_slot, to_slot, _, target) in enumerate(sends):

        @pl.when(cond)
        def _():
            kv_copy(
                jnp.maximum(from_slot, 0), jnp.maximum(to_slot, 0), number, target
            ).wait_send()

    for p in range(pieces):
        x_copy(p).wait_send()
        t_copy(p).wait_send()
        h_copy(p).wait_send()

        @pl.when(has_next)
        def _():
            s_copy(p).wait_send()

    for hop in range(1, n_head):
        p_copy(hop).wait_send()


def local(
    n_seq,
    n_head,
    query_rows,
    key_rows,
    value_rows,
    rates,
    fw_decay,
    fw_step,
    fast_gate,
    fast_up,
    fast_down,
    ttt_gain,
    attn_gain,
    out_proj,
):
    rows, cols = query_rows.shape
    heads, dim, fast = fast_gate.shape
    width = out_proj.shape[1]
    share = rows // n_head
    mats = 3 * heads
    slots = WINDOW // rows + GROUP
    dma = pltpu.SemaphoreType.DMA
    pieces = mats * SPLIT
    chunk = dim // 2 // SPLIT
    piece = pltpu.VMEM((pieces, chunk, fast), BF)
    moved = pl.BlockSpec(memory_space=pl.ANY)
    small = pl.BlockSpec(memory_space=pltpu.VMEM)
    return pl.pallas_call(
        functools.partial(kernel, n_seq, n_head),
        out_shape=jax.ShapeDtypeStruct((share, width), BF),
        in_specs=[moved] * 3 + [small] * 3 + [moved] * 3 + [small] * 2 + [moved],
        out_specs=pl.BlockSpec(memory_space=pltpu.VMEM),
        scratch_shapes=[
            pltpu.VMEM((rows, cols), BF),
            pltpu.VMEM((heads, dim, fast), F32),
            pltpu.VMEM((heads, dim, fast), F32),
            pltpu.VMEM((heads, dim, fast), F32),
            pltpu.VMEM((cols, width), BF),
            pltpu.VMEM((slots, 2, rows, cols), BF),
            pltpu.VMEM((8, 128), F32),
            pltpu.VMEM((8, 128), F32),
            pltpu.VMEM((8, 128), F32),
            pltpu.VMEM((8, 128), F32),
            pltpu.VMEM((mats, dim, fast), F32),
            piece,
            piece,
            pltpu.VMEM((pieces, chunk, fast), F32),
            piece,
            piece,
            piece,
            piece,
            piece,
            piece,
            pltpu.VMEM((mats, dim, fast), F32),
            pltpu.VMEM((heads, rows, 256), BF),
            pltpu.VMEM((heads, rows, 256), F32),
            pltpu.VMEM((heads, rows, 128), F32),
            pltpu.VMEM((heads, rows, 128), F32),
            pltpu.VMEM((heads, rows, dim), F32),
            pltpu.VMEM((heads, rows, dim), BF),
            pltpu.VMEM((heads, rows, 128), F32),
            pltpu.VMEM((heads, rows, dim), BF),
            pltpu.VMEM((n_head - 1, share, width), BF),
            pltpu.VMEM((n_head - 1, share, width), BF),
            dma((7,)),
            dma((10,)),
            dma((slots,)),
            dma((4,)),
            dma((pieces,)),
            dma((pieces,)),
            dma((pieces,)),
            dma((pieces,)),
            dma((pieces,)),
            dma((pieces,)),
            dma((pieces,)),
            dma((pieces,)),
            dma((n_head - 1,)),
            dma((n_head - 1,)),
        ],
        compiler_params=pltpu.CompilerParams(
            collective_id=0, has_side_effects=True, vmem_limit_bytes=56 * 1024 * 1024
        ),
    )(
        query_rows,
        key_rows,
        value_rows,
        rates.T,
        fw_decay,
        fw_step.reshape(1, -1),
        fast_gate,
        fast_up,
        jnp.swapaxes(fast_down, 1, 2),
        ttt_gain,
        attn_gain,
        out_proj,
    )


def solution(mesh):
    in_specs = (
        P("seq", "head"),
        P("seq", "head"),
        P("seq", "head"),
        P("seq", "head"),
        P("seq", "head"),
        P("head"),
        P("head", None, None),
        P("head", None, None),
        P("head", None, None),
        P("head"),
        P("head"),
        P("head", None),
    )
    out_specs = P(("seq", "head"), None)
    body = functools.partial(local, mesh.shape["seq"], mesh.shape["head"])
    return jax.shard_map(body, mesh=mesh, in_specs=in_specs, out_specs=out_specs, check_vma=False)
```

```python
import functools
import math

import jax
import jax.numpy as jnp
from jax import lax
from jax.experimental import pallas as pl
from jax.experimental.pallas import tpu as pltpu
from jax.sharding import PartitionSpec as P

WINDOW = 2048
NS_STEPS = 5
GROUP = 4
SPLIT = 2
MESH = pl.DeviceIdType.MESH
BF = jnp.bfloat16
F32 = jnp.float32
coef_a = 3.4445
coef_b = -4.775
coef_c = 2.0315
FAR = -1e30

NN = (((1,), (0,)), ((), ()))
NT = (((1,), (1,)), ((), ()))


def dot1(left, right, dims=NN):
    return lax.dot_general(left, right, dims, preferred_element_type=F32)


def halves(value):
    high = value.astype(BF)
    return high, (value - high.astype(F32)).astype(BF)


def dot3(left, right, dims=NN):
    return dot1(left[0], right[0], dims) + (
        dot1(left[0], right[1], dims) + dot1(left[1], right[0], dims)
    )


def dot2(left, right):
    return dot1(left, right[0]) + dot1(left, right[1])


def rms_inverse(values):
    return lax.rsqrt(jnp.mean(values * values, axis=-1, keepdims=True) + 1e-06)


def rms_rows(values):
    return values * rms_inverse(values)


def kernel(
    n_seq,
    n_head,
    q_hbm,
    k_hbm,
    v_hbm,
    rates_ref,
    decay_ref,
    step_ref,
    gate_hbm,
    up_hbm,
    downt_hbm,
    tgain_ref,
    again_ref,
    proj_hbm,
    out_ref,
    q_ref,
    gate_ref,
    up_ref,
    downt,
    proj_ref,
    kv,
    dec_own,
    dec_sib,
    dec_chip,
    dec_across,
    upd,
    x_out,
    x_in,
    t_own,
    t_out,
    t_in,
    s_out,
    s_in,
    h_out,
    h_in,
    state,
    qpad,
    acc,
    top,
    total,
    share_attn,
    query_low,
    query_scale,
    mixed,
    p_out,
    p_in,
    load_sems,
    kv_send,
    kv_recv,
    dec_sems,
    x_send,
    x_recv,
    t_send,
    t_recv,
    s_send,
    s_recv,
    y_send,
    h_send,
    h_recv,
    p_send,
    p_recv,
):
    rows = q_ref.shape[0]
    heads, dim, _ = gate_ref.shape
    part = dim // 2
    chunk = part // SPLIT
    pieces = 3 * heads * SPLIT
    scale = 1.0 / math.sqrt(dim)
    reach = WINDOW // rows
    n_group = n_seq // GROUP
    me = lax.axis_index("seq")
    head = lax.axis_index("head")
    group = me // GROUP
    member = me % GROUP
    side = member // 2
    core = member % 2
    sibling = me + 1 - 2 * core
    across = me + 2 - 4 * side
    onward = me + GROUP
    own = reach + member

    loads = [
        pltpu.make_async_copy(source, target, load_sems.at[i])
        for i, (source, target) in enumerate(
            (
                (k_hbm, kv.at[own, 0]),
                (v_hbm, kv.at[own, 1]),
                (gate_hbm, gate_ref),
                (up_hbm, up_ref),
                (downt_hbm, downt),
                (q_hbm, q_ref),
                (proj_hbm, proj_ref),
            )
        )
    ]
    for load in loads:
        load.start()

    barrier = pltpu.get_barrier_semaphore()

    def greet(seq_pos, head_pos):
        pl.semaphore_signal(barrier, inc=1, device_id=(seq_pos, head_pos), device_id_type=MESH)

    greet(sibling, head)
    greet(across, head)
    expected = jnp.int32(2 + n_head - 1)
    for step in (GROUP, -GROUP):
        there = (me + step >= 0) & (me + step < n_seq)
        pl.when(there)(functools.partial(greet, me + step, head))
        expected = expected + there.astype(jnp.int32)
    for hop in range(1, n_head):
        greet(me, lax.rem(head + hop, n_head))

    dec_own[...] = jnp.zeros(dec_own.shape, F32)
    for h in range(heads):
        dec_own[h : h + 1, :] = jnp.broadcast_to(decay_ref[0:1, h : h + 1], (1, 128))
    loads[0].wait()
    loads[1].wait()
    pl.semaphore_wait(barrier, expected)

    def kv_copy(from_slot, to_slot, number, seq_pos):
        return pltpu.make_async_remote_copy(
            src_ref=kv.at[from_slot],
            dst_ref=kv.at[to_slot],
            send_sem=kv_send.at[number],
            recv_sem=kv_recv.at[to_slot],
            device_id=(seq_pos, head),
            device_id_type=MESH,
        )

    def slot_of(distance):
        return reach + member - distance

    has_next = group + 1 < n_group
    sends = [
        (has_next, own, own - GROUP, 0, onward),
        (side == 0, own, own, 1, across),
        (core == 0, own, own, 2, sibling),
        (has_next & (me >= 4), slot_of(4), slot_of(8), 3, onward),
        (me >= 4, slot_of(4), slot_of(4), 4, across),
        (me >= 4, slot_of(4), slot_of(4), 5, sibling),
        (has_next & (me >= 4) & (side == 0), slot_of(2), slot_of(6), 6, onward),
        ((me >= 8) & (core == 1), slot_of(8), slot_of(8), 7, sibling),
        (me >= 2, slot_of(2), slot_of(2), 8, sibling),
        (me >= 6, slot_of(6), slot_of(6), 9, sibling),
    ]

    def start_send(number):
        cond, from_slot, to_slot, _, target = sends[number]

        @pl.when(cond)
        def _():
            kv_copy(jnp.maximum(from_slot, 0), jnp.maximum(to_slot, 0), number, target).start()

    def await_block(distance):
        slot = slot_of(distance)
        pltpu.make_async_copy(kv.at[slot], kv.at[slot], kv_recv.at[slot]).wait()

    def arrive(distance, numbers):
        @pl.when(me >= distance)
        def _():
            await_block(distance)
            for number in numbers:
                start_send(number)

    dec_copy = pltpu.make_async_remote_copy(
        src_ref=dec_own,
        dst_ref=dec_sib,
        send_sem=dec_sems.at[0],
        recv_sem=dec_sems.at[1],
        device_id=(sibling, head),
        device_id_type=MESH,
    )
    dec_copy.start()
    for number in (0, 1, 2):
        start_send(number)

    for load in loads[2:5]:
        load.wait()

    mine_at = pl.multiple_of(core * part, part)
    other_at = pl.multiple_of((1 - core) * part, part)

    def pair_copy(source, target, send, recv, j, seq_pos):
        return pltpu.make_async_remote_copy(
            src_ref=source.at[j],
            dst_ref=target.at[j],
            send_sem=send.at[j],
            recv_sem=recv.at[j],
            device_id=(seq_pos, head),
            device_id_type=MESH,
        )

    x_copy = lambda p: pair_copy(x_out, x_in, x_send, x_recv, p, sibling)
    t_copy = lambda p: pair_copy(t_out, t_in, t_send, t_recv, p, across)
    s_copy = lambda p: pair_copy(s_out, s_in, s_send, s_recv, p, onward)
    y_copy = lambda p: pair_copy(s_in, s_in, y_send, s_recv, p, across)
    h_copy = lambda p: pair_copy(h_out, h_in, h_send, h_recv, p, sibling)

    def rows_at(p, base):
        return pl.ds(pl.multiple_of(base + (p % SPLIT) * chunk, chunk), chunk)

    @pl.when(group == 0)
    def _():
        s_in[...] = jnp.zeros(s_in.shape, BF)

    @pl.when(side == 0)
    def _():
        t_in[...] = jnp.zeros(t_in.shape, BF)

    first = core == 0

    def of_pair(p):
        j = p // SPLIT
        h = j // 3
        d_own = dec_own[pl.ds(h, 1), :][:, 0:1]
        d_sib = dec_sib[pl.ds(h, 1), :][:, 0:1]
        u_own = upd[j, rows_at(p, mine_at), :]
        u_sib = x_in[p].astype(F32)
        return (
            jnp.where(first, d_own, d_sib),
            jnp.where(first, d_sib, d_own),
            jnp.where(first, u_own, u_sib),
            jnp.where(first, u_sib, u_own),
        )

    def sum_pair(p, carry):
        x_copy(p).wait_recv()
        _, decay1, u0, u1 = of_pair(p)
        both = decay1 * u0 + u1
        t_own[p] = both

        @pl.when(side == 0)
        def _():
            t_out[p] = both.astype(BF)
            t_copy(p).start()

        return carry

    per_head = 3 * SPLIT

    def sum_pairs(h):
        lax.fori_loop(h * per_head, (h + 1) * per_head, sum_pair, 0)

    def gradients(h):
        cols = slice(h * dim, (h + 1) * dim)
        key = kv[own, 0].astype(F32)[:, cols]
        value = kv[own, 1].astype(F32)[:, cols]
        key_scale = rms_inverse(key)
        rate = -jnp.broadcast_to(rates_ref[h : h + 1, :], (8, rows)).T[:, 0:1]
        key_low = key.astype(BF)
        pre_gate = key_scale * dot2(key_low, halves(gate_ref[h]))
        pre_up = key_scale * dot2(key_low, halves(up_ref[h]))
        sig = jax.nn.sigmoid(pre_gate)
        active = pre_gate * sig
        back = (rate * key_scale) * dot2(value.astype(BF), halves(downt[h]))
        key_t = key.T.astype(BF)
        grads = (
            dot2(key_t, halves(back * pre_up * (sig * (1.0 + pre_gate * (1.0 - sig))))),
            dot2(key_t, halves(back * active)),
            dot2(value.T.astype(BF), halves(rate * active * pre_up)),
        )
        for i, grad in enumerate(grads):
            size = jnp.sum(jnp.sum(grad * grad, axis=1, keepdims=True), axis=0, keepdims=True)
            upd[3 * h + i] = grad / (jnp.sqrt(size) + 1e-07)

    def orthogonalize(h):
        def sweep(turn, carry):
            for j in range(3 * h, 3 * h + 3):
                current = upd[j]
                low = current.astype(BF)
                gram = dot1(low, low, NT)
                gram_low = gram.astype(BF)
                poly = coef_b * gram + coef_c * dot1(gram_low, gram_low)
                upd[j] = coef_a * current + dot1(poly.astype(BF), low)
            return carry

        lax.fori_loop(0, NS_STEPS, sweep, 0)
        for p in range(h * per_head, (h + 1) * per_head):
            j = p // SPLIT
            if p % SPLIT == 0:
                upd[j] = -step_ref[0:1, h : h + 1] * upd[j]
            x_out[p] = upd[j, rows_at(p, other_at), :].astype(BF)
            x_copy(p).start()

    near = side == 0

    def chain(head_id):
        def link(p, carry):
            h = p // SPLIT // 3
            @pl.when(side == 1)
            def _():
                t_copy(p).wait_recv()

            @pl.when(group > 0)
            def _():
                s_copy(p).wait_recv()

            @pl.when((group > 0) & (side == 1))
            def _():
                y_copy(p).start()

            c_own = dec_chip[pl.ds(h, 1), :][:, 0:1]
            c_far = dec_across[pl.ds(h, 1), :][:, 0:1]
            chip0 = jnp.where(near, c_own, c_far)
            chip1 = jnp.where(near, c_far, c_own)
            t_far = t_in[p].astype(F32)
            t_mine = t_own[p]
            t0 = jnp.where(near, t_mine, t_far)
            t1 = jnp.where(near, t_far, t_mine)
            enter = s_in[p].astype(F32)
            halfway = chip0 * enter + t0

            @pl.when(has_next & (side == 1))
            def _():
                s_out[p] = (chip1 * halfway + t1).astype(BF)
                s_copy(p).start()

            decay0, _, u0, _ = of_pair(p)
            before = jnp.where(near, enter, halfway)
            middle = decay0 * before + u0
            h_out[p] = jnp.where(first, middle, before).astype(BF)
            h_copy(p).start()
            state[p // SPLIT, rows_at(p, mine_at), :] = jnp.where(first, before, middle)
            return carry

        lax.fori_loop(head_id * per_head, (head_id + 1) * per_head, link, 0)

    for h in range(heads):
        gradients(h)
        if h == 1:
            pl.when(side == 1)(lambda: arrive(2, (8,)))
        if h == 0:
            dec_copy.wait()
            dec_chip[...] = dec_own[...] * dec_sib[...]
            dec_chip_copy = pltpu.make_async_remote_copy(
                src_ref=dec_chip,
                dst_ref=dec_across,
                send_sem=dec_sems.at[2],
                recv_sem=dec_sems.at[3],
                device_id=(across, head),
                device_id_type=MESH,
            )
            dec_chip_copy.start()
        else:
            if h == 1:
                dec_chip_copy.wait()
            sum_pairs(h - 1)
        orthogonalize(h)
        if h == 0:
            arrive(4, (3, 4, 5))
    pl.when((group == 0) & (side == 1))(lambda: chain(0))
    sum_pairs(heads - 1)
    pl.when(side == 0)(lambda: arrive(2, (6, 8)))
    arrive(8, (7,))

    loads[5].wait()
    lane = lax.broadcasted_iota(jnp.int32, (rows, 256), 1)
    starts = [0, heads * dim - 256]
    for h in range(heads):
        begin = h * dim - starts[h]
        inside = (lane >= begin) & (lane < begin + dim)
        wide = q_ref[:, starts[h] : starts[h] + 256].astype(F32)
        qpad[h] = jnp.where(inside, wide, 0.0).astype(BF)
    acc[...] = jnp.zeros(acc.shape, F32)
    top[...] = jnp.full(top.shape, FAR, F32)
    total[...] = jnp.zeros(total.shape, F32)
    gap = lax.broadcasted_iota(jnp.int32, (rows, rows), 0) - lax.broadcasted_iota(
        jnp.int32, (rows, rows), 1
    )

    def attend(distance):
        slot = slot_of(distance)
        back = gap + distance * rows
        for h in range(heads):
            cols = slice(starts[h], starts[h] + 256)
            scores = dot1(qpad[h], kv[slot, 0, :, cols], NT) * scale
            if distance == 0:
                scores = jnp.where(back >= 0, scores, FAR)
            if distance == reach:
                scores = jnp.where(back < WINDOW, scores, FAR)
            old_top = top[h][:, 0:1]
            new_top = jnp.maximum(old_top, jnp.max(scores, axis=1, keepdims=True))
            weights = jnp.exp(scores - new_top)
            shrink = jnp.exp(old_top - new_top)
            total[h] = jnp.broadcast_to(
                total[h][:, 0:1] * shrink + jnp.sum(weights, axis=1, keepdims=True), (rows, 128)
            )
            acc[h] = acc[h] * shrink + dot1(weights.astype(BF), kv[slot, 1, :, cols])
            top[h] = jnp.broadcast_to(new_top, (rows, 128))

    def turn_of(distance):
        if distance % 2 == 1:
            await_block(distance)
        attend(distance)

    last_at = {0: 2, 1: 6}

    def rest():
        for h in range(1, heads):
            chain(h)

    for position, distance in enumerate((0, 1, 3, 2, 4, 8, 7, 5, 6)):
        if position == 6:
            arrive(6, (9,))
        if position in (2, 4, 6, 8) and position // 2 < n_group:
            pl.when((group == position // 2) & (side == 1))(lambda: chain(0))
        for g, at in last_at.items():
            if at == position:
                pl.when((group == g) & (side == 1))(rest)
        pl.when(me >= distance)(functools.partial(turn_of, distance))

    for h in range(heads):
        cols = slice(h * dim, (h + 1) * dim)
        begin = h * dim - starts[h]
        attended = acc[h][:, begin : begin + dim] / total[h][:, 0:1]
        share_attn[h] = rms_rows(attended) * again_ref[...].reshape(1, -1)[:, cols]
        query = q_ref[...].astype(F32)[:, cols]
        query_low[h] = query.astype(BF)
        query_scale[h] = jnp.broadcast_to(rms_inverse(query), (rows, 128))

    pl.when((group > 4) | (side == 0))(lambda: chain(0))

    pl.when((group > 1) & has_next & (side == 1))(rest)
    loads[6].wait()
    for h in range(heads):
        if h == 1:
            pl.when((side == 0) | ((group > 1) & (group + 1 == n_group)))(rest)
        for p in range(h * per_head, (h + 1) * per_head):
            h_copy(p).wait_recv()
            state[p // SPLIT, rows_at(p, other_at), :] = h_in[p].astype(F32)
        cols = slice(h * dim, (h + 1) * dim)
        query = query_low[h]
        scale_q = query_scale[h][:, 0:1]
        pre_gate = scale_q * dot2(query, halves(gate_ref[h] + state[3 * h]))
        pre_up = scale_q * dot2(query, halves(up_ref[h] + state[3 * h + 1]))
        hidden = pre_gate * jax.nn.sigmoid(pre_gate) * pre_up
        applied = dot3(halves(hidden), halves(downt[h] + state[3 * h + 2]), NT)
        mixed[h] = (
            rms_rows(applied) * tgain_ref[...].reshape(1, -1)[:, cols] + share_attn[h]
        ).astype(BF)

    share = rows // n_head

    def project(target):
        at = pl.multiple_of(target * share, share)
        result = dot1(mixed[0, pl.ds(at, share), :], proj_ref[0:dim, :])
        for h in range(1, heads):
            result = result + dot1(
                mixed[h, pl.ds(at, share), :], proj_ref[h * dim : (h + 1) * dim, :]
            )
        return result

    def p_copy(hop):
        return pltpu.make_async_remote_copy(
            src_ref=p_out.at[hop - 1],
            dst_ref=p_in.at[hop - 1],
            send_sem=p_send.at[hop - 1],
            recv_sem=p_recv.at[hop - 1],
            device_id=(me, lax.rem(head + hop, n_head)),
            device_id_type=MESH,
        )

    for hop in range(1, n_head):
        p_out[hop - 1] = project(lax.rem(head + hop, n_head)).astype(BF)
        p_copy(hop).start()
    result = project(head)
    for hop in range(1, n_head):
        p_copy(hop).wait_recv()
        result = result + p_in[hop - 1].astype(F32)
    out_ref[...] = result.astype(BF)

    for number, (cond, from_slot, to_slot, _, target) in enumerate(sends):

        @pl.when(cond)
        def _():
            kv_copy(
                jnp.maximum(from_slot, 0), jnp.maximum(to_slot, 0), number, target
            ).wait_send()

    for p in range(pieces):
        x_copy(p).wait_send()
        h_copy(p).wait_send()

        @pl.when(side == 0)
        def _():
            t_copy(p).wait_send()

        @pl.when((group > 0) & (side == 1))
        def _():
            y_copy(p).wait_send()

        @pl.when(has_next & (side == 1))
        def _():
            s_copy(p).wait_send()

    for hop in range(1, n_head):
        p_copy(hop).wait_send()


def local(
    n_seq,
    n_head,
    query_rows,
    key_rows,
    value_rows,
    rates,
    fw_decay,
    fw_step,
    fast_gate,
    fast_up,
    fast_down,
    ttt_gain,
    attn_gain,
    out_proj,
):
    rows, cols = query_rows.shape
    heads, dim, fast = fast_gate.shape
    width = out_proj.shape[1]
    share = rows // n_head
    mats = 3 * heads
    slots = WINDOW // rows + GROUP
    dma = pltpu.SemaphoreType.DMA
    pieces = mats * SPLIT
    chunk = dim // 2 // SPLIT
    piece = pltpu.VMEM((pieces, chunk, fast), BF)
    moved = pl.BlockSpec(memory_space=pl.ANY)
    small = pl.BlockSpec(memory_space=pltpu.VMEM)
    return pl.pallas_call(
        functools.partial(kernel, n_seq, n_head),
        out_shape=jax.ShapeDtypeStruct((share, width), BF),
        in_specs=[moved] * 3 + [small] * 3 + [moved] * 3 + [small] * 2 + [moved],
        out_specs=pl.BlockSpec(memory_space=pltpu.VMEM),
        scratch_shapes=[
            pltpu.VMEM((rows, cols), BF),
            pltpu.VMEM((heads, dim, fast), F32),
            pltpu.VMEM((heads, dim, fast), F32),
            pltpu.VMEM((heads, dim, fast), F32),
            pltpu.VMEM((cols, width), BF),
            pltpu.VMEM((slots, 2, rows, cols), BF),
            pltpu.VMEM((8, 128), F32),
            pltpu.VMEM((8, 128), F32),
            pltpu.VMEM((8, 128), F32),
            pltpu.VMEM((8, 128), F32),
            pltpu.VMEM((mats, dim, fast), F32),
            piece,
            piece,
            pltpu.VMEM((pieces, chunk, fast), F32),
            piece,
            piece,
            piece,
            piece,
            piece,
            piece,
            pltpu.VMEM((mats, dim, fast), F32),
            pltpu.VMEM((heads, rows, 256), BF),
            pltpu.VMEM((heads, rows, 256), F32),
            pltpu.VMEM((heads, rows, 128), F32),
            pltpu.VMEM((heads, rows, 128), F32),
            pltpu.VMEM((heads, rows, dim), F32),
            pltpu.VMEM((heads, rows, dim), BF),
            pltpu.VMEM((heads, rows, 128), F32),
            pltpu.VMEM((heads, rows, dim), BF),
            pltpu.VMEM((n_head - 1, share, width), BF),
            pltpu.VMEM((n_head - 1, share, width), BF),
            dma((7,)),
            dma((10,)),
            dma((slots,)),
            dma((4,)),
            dma((pieces,)),
            dma((pieces,)),
            dma((pieces,)),
            dma((pieces,)),
            dma((pieces,)),
            dma((pieces,)),
            dma((pieces,)),
            dma((pieces,)),
            dma((pieces,)),
            dma((n_head - 1,)),
            dma((n_head - 1,)),
        ],
        compiler_params=pltpu.CompilerParams(
            collective_id=0, has_side_effects=True, vmem_limit_bytes=56 * 1024 * 1024
        ),
    )(
        query_rows,
        key_rows,
        value_rows,
        rates.T,
        fw_decay,
        fw_step.reshape(1, -1),
        fast_gate,
        fast_up,
        jnp.swapaxes(fast_down, 1, 2),
        ttt_gain,
        attn_gain,
        out_proj,
    )


def solution(mesh):
    in_specs = (
        P("seq", "head"),
        P("seq", "head"),
        P("seq", "head"),
        P("seq", "head"),
        P("seq", "head"),
        P("head"),
        P("head", None, None),
        P("head", None, None),
        P("head", None, None),
        P("head"),
        P("head"),
        P("head", None),
    )
    out_specs = P(("seq", "head"), None)
    body = functools.partial(local, mesh.shape["seq"], mesh.shape["head"])
    return jax.shard_map(body, mesh=mesh, in_specs=in_specs, out_specs=out_specs, check_vma=False)
```

```python
import functools
import math

import jax
import jax.numpy as jnp
from jax import lax
from jax.experimental import pallas as pl
from jax.experimental.pallas import tpu as pltpu
from jax.sharding import PartitionSpec as P

WINDOW = 2048
NS_STEPS = 5
GROUP = 4
SPLIT = 2
MESH = pl.DeviceIdType.MESH
BF = jnp.bfloat16
F32 = jnp.float32
coef_a = 3.4445
coef_b = -4.775
coef_c = 2.0315
FAR = -1e30

NN = (((1,), (0,)), ((), ()))
NT = (((1,), (1,)), ((), ()))


def dot1(left, right, dims=NN):
    return lax.dot_general(left, right, dims, preferred_element_type=F32)


def halves(value):
    high = value.astype(BF)
    return high, (value - high.astype(F32)).astype(BF)


def dot3(left, right, dims=NN):
    return dot1(left[0], right[0], dims) + (
        dot1(left[0], right[1], dims) + dot1(left[1], right[0], dims)
    )


def dot2(left, right):
    return dot1(left, right[0]) + dot1(left, right[1])


def rms_inverse(values):
    return lax.rsqrt(jnp.mean(values * values, axis=-1, keepdims=True) + 1e-06)


def rms_rows(values):
    return values * rms_inverse(values)


def kernel(
    n_seq,
    n_head,
    q_hbm,
    k_hbm,
    v_hbm,
    rates_ref,
    decay_ref,
    step_ref,
    gate_hbm,
    up_hbm,
    downt_hbm,
    tgain_ref,
    again_ref,
    proj_hbm,
    out_ref,
    q_ref,
    gate_ref,
    up_ref,
    downt,
    proj_ref,
    kv,
    dec_own,
    dec_sib,
    dec_chip,
    dec_across,
    upd,
    x_out,
    x_in,
    t_own,
    t_out,
    t_in,
    s_out,
    s_in,
    h_out,
    h_in,
    state,
    qpad,
    acc,
    top,
    total,
    share_attn,
    query_low,
    query_scale,
    mixed,
    p_out,
    p_in,
    load_sems,
    kv_send,
    kv_recv,
    dec_sems,
    x_send,
    x_recv,
    t_send,
    t_recv,
    s_send,
    s_recv,
    y_send,
    h_send,
    h_recv,
    p_send,
    p_recv,
):
    rows = q_ref.shape[0]
    heads, dim, _ = gate_ref.shape
    part = dim // 2
    chunk = part // SPLIT
    pieces = 3 * heads * SPLIT
    scale = 1.0 / math.sqrt(dim)
    reach = WINDOW // rows
    n_group = n_seq // GROUP
    me = lax.axis_index("seq")
    head = lax.axis_index("head")
    group = me // GROUP
    member = me % GROUP
    side = member // 2
    core = member % 2
    sibling = me + 1 - 2 * core
    across = me + 2 - 4 * side
    onward = me + GROUP
    own = reach + member

    loads = [
        pltpu.make_async_copy(source, target, load_sems.at[i])
        for i, (source, target) in enumerate(
            (
                (k_hbm, kv.at[own, 0]),
                (v_hbm, kv.at[own, 1]),
                (gate_hbm, gate_ref),
                (up_hbm, up_ref),
                (downt_hbm, downt),
                (q_hbm, q_ref),
                (proj_hbm, proj_ref),
            )
        )
    ]
    for load in loads:
        load.start()

    barrier = pltpu.get_barrier_semaphore()

    def greet(seq_pos, head_pos):
        pl.semaphore_signal(barrier, inc=1, device_id=(seq_pos, head_pos), device_id_type=MESH)

    greet(sibling, head)
    greet(across, head)
    expected = jnp.int32(2 + n_head - 1)
    for step in (GROUP, -GROUP):
        there = (me + step >= 0) & (me + step < n_seq)
        pl.when(there)(functools.partial(greet, me + step, head))
        expected = expected + there.astype(jnp.int32)
    for hop in range(1, n_head):
        greet(me, lax.rem(head + hop, n_head))

    dec_own[...] = jnp.zeros(dec_own.shape, F32)
    for h in range(heads):
        dec_own[h : h + 1, :] = jnp.broadcast_to(decay_ref[0:1, h : h + 1], (1, 128))
    loads[0].wait()
    loads[1].wait()
    pl.semaphore_wait(barrier, expected)

    def kv_copy(from_slot, to_slot, number, seq_pos):
        return pltpu.make_async_remote_copy(
            src_ref=kv.at[from_slot],
            dst_ref=kv.at[to_slot],
            send_sem=kv_send.at[number],
            recv_sem=kv_recv.at[to_slot],
            device_id=(seq_pos, head),
            device_id_type=MESH,
        )

    def slot_of(distance):
        return reach + member - distance

    has_next = group + 1 < n_group
    sends = [
        (has_next, own, own - GROUP, 0, onward),
        (side == 0, own, own, 1, across),
        (core == 0, own, own, 2, sibling),
        (has_next & (me >= 4), slot_of(4), slot_of(8), 3, onward),
        (me >= 4, slot_of(4), slot_of(4), 4, across),
        (me >= 4, slot_of(4), slot_of(4), 5, sibling),
        (has_next & (me >= 4) & (side == 0), slot_of(2), slot_of(6), 6, onward),
        ((me >= 8) & (core == 1), slot_of(8), slot_of(8), 7, sibling),
        (me >= 2, slot_of(2), slot_of(2), 8, sibling),
        (me >= 6, slot_of(6), slot_of(6), 9, sibling),
    ]

    def start_send(number):
        cond, from_slot, to_slot, _, target = sends[number]

        @pl.when(cond)
        def _():
            kv_copy(jnp.maximum(from_slot, 0), jnp.maximum(to_slot, 0), number, target).start()

    def await_block(distance):
        slot = slot_of(distance)
        pltpu.make_async_copy(kv.at[slot], kv.at[slot], kv_recv.at[slot]).wait()

    def arrive(distance, numbers):
        @pl.when(me >= distance)
        def _():
            await_block(distance)
            for number in numbers:
                start_send(number)

    dec_copy = pltpu.make_async_remote_copy(
        src_ref=dec_own,
        dst_ref=dec_sib,
        send_sem=dec_sems.at[0],
        recv_sem=dec_sems.at[1],
        device_id=(sibling, head),
        device_id_type=MESH,
    )
    dec_copy.start()
    for number in (0, 1, 2):
        start_send(number)

    for load in loads[2:5]:
        load.wait()

    mine_at = pl.multiple_of(core * part, part)
    other_at = pl.multiple_of((1 - core) * part, part)

    def pair_copy(source, target, send, recv, j, seq_pos):
        return pltpu.make_async_remote_copy(
            src_ref=source.at[j],
            dst_ref=target.at[j],
            send_sem=send.at[j],
            recv_sem=recv.at[j],
            device_id=(seq_pos, head),
            device_id_type=MESH,
        )

    x_copy = lambda p: pair_copy(x_out, x_in, x_send, x_recv, p, sibling)
    t_copy = lambda p: pair_copy(t_out, t_in, t_send, t_recv, p, across)
    s_copy = lambda p: pair_copy(s_out, s_in, s_send, s_recv, p, onward)
    y_copy = lambda p: pair_copy(s_in, s_in, y_send, s_recv, p, across)
    h_copy = lambda p: pair_copy(h_out, h_in, h_send, h_recv, p, sibling)

    def rows_at(p, base):
        return pl.ds(pl.multiple_of(base + (p % SPLIT) * chunk, chunk), chunk)

    @pl.when(group == 0)
    def _():
        s_in[...] = jnp.zeros(s_in.shape, BF)

    @pl.when(side == 0)
    def _():
        t_in[...] = jnp.zeros(t_in.shape, BF)

    first = core == 0

    def of_pair(p):
        j = p // SPLIT
        h = j // 3
        d_own = dec_own[pl.ds(h, 1), :][:, 0:1]
        d_sib = dec_sib[pl.ds(h, 1), :][:, 0:1]
        u_own = upd[j, rows_at(p, mine_at), :]
        u_sib = x_in[p].astype(F32)
        return (
            jnp.where(first, d_own, d_sib),
            jnp.where(first, d_sib, d_own),
            jnp.where(first, u_own, u_sib),
            jnp.where(first, u_sib, u_own),
        )

    def sum_pair(p, carry):
        x_copy(p).wait_recv()
        _, decay1, u0, u1 = of_pair(p)
        both = decay1 * u0 + u1
        t_own[p] = both

        @pl.when(side == 0)
        def _():
            t_out[p] = both.astype(BF)
            t_copy(p).start()

        return carry

    per_head = 3 * SPLIT

    def sum_pairs(h):
        lax.fori_loop(h * per_head, (h + 1) * per_head, sum_pair, 0)

    def gradients(h):
        cols = slice(h * dim, (h + 1) * dim)
        key = kv[own, 0].astype(F32)[:, cols]
        value = kv[own, 1].astype(F32)[:, cols]
        key_scale = rms_inverse(key)
        rate = -jnp.broadcast_to(rates_ref[h : h + 1, :], (8, rows)).T[:, 0:1]
        key_low = key.astype(BF)
        pre_gate = key_scale * dot2(key_low, halves(gate_ref[h]))
        pre_up = key_scale * dot2(key_low, halves(up_ref[h]))
        sig = jax.nn.sigmoid(pre_gate)
        active = pre_gate * sig
        back = (rate * key_scale) * dot2(value.astype(BF), halves(downt[h]))
        key_t = key.T.astype(BF)
        grads = (
            dot2(key_t, halves(back * pre_up * (sig * (1.0 + pre_gate * (1.0 - sig))))),
            dot2(key_t, halves(back * active)),
            dot2(value.T.astype(BF), halves(rate * active * pre_up)),
        )
        for i, grad in enumerate(grads):
            size = jnp.sum(jnp.sum(grad * grad, axis=1, keepdims=True), axis=0, keepdims=True)
            upd[3 * h + i] = grad / (jnp.sqrt(size) + 1e-07)

    def orthogonalize(h):
        def sweep(turn, carry):
            for j in range(3 * h, 3 * h + 3):
                current = upd[j]
                low = current.astype(BF)
                gram = dot1(low, low, NT)
                gram_low = gram.astype(BF)
                poly = coef_b * gram + coef_c * dot1(gram_low, gram_low)
                upd[j] = coef_a * current + dot1(poly.astype(BF), low)
            return carry

        lax.fori_loop(0, NS_STEPS, sweep, 0)
        for p in range(h * per_head, (h + 1) * per_head):
            j = p // SPLIT
            if p % SPLIT == 0:
                upd[j] = -step_ref[0:1, h : h + 1] * upd[j]
            x_out[p] = upd[j, rows_at(p, other_at), :].astype(BF)
            x_copy(p).start()

    near = side == 0

    def chain(head_id):
        def link(p, carry):
            h = p // SPLIT // 3
            @pl.when(side == 1)
            def _():
                t_copy(p).wait_recv()

            @pl.when(group > 0)
            def _():
                s_copy(p).wait_recv()

            @pl.when((group > 0) & (side == 1))
            def _():
                y_copy(p).start()

            c_own = dec_chip[pl.ds(h, 1), :][:, 0:1]
            c_far = dec_across[pl.ds(h, 1), :][:, 0:1]
            chip0 = jnp.where(near, c_own, c_far)
            chip1 = jnp.where(near, c_far, c_own)
            t_far = t_in[p].astype(F32)
            t_mine = t_own[p]
            t0 = jnp.where(near, t_mine, t_far)
            t1 = jnp.where(near, t_far, t_mine)
            enter = s_in[p].astype(F32)
            halfway = chip0 * enter + t0

            @pl.when(has_next & (side == 1))
            def _():
                s_out[p] = (chip1 * halfway + t1).astype(BF)
                s_copy(p).start()

            decay0, _, u0, _ = of_pair(p)
            before = jnp.where(near, enter, halfway)
            middle = decay0 * before + u0
            h_out[p] = jnp.where(first, middle, before).astype(BF)
            h_copy(p).start()
            state[p // SPLIT, rows_at(p, mine_at), :] = jnp.where(first, before, middle)
            return carry

        lax.fori_loop(head_id * per_head, (head_id + 1) * per_head, link, 0)

    for h in range(heads):
        gradients(h)
        if h == 1:
            pl.when(side == 1)(lambda: arrive(2, (8,)))
        if h == 0:
            dec_copy.wait()
            dec_chip[...] = dec_own[...] * dec_sib[...]
            dec_chip_copy = pltpu.make_async_remote_copy(
                src_ref=dec_chip,
                dst_ref=dec_across,
                send_sem=dec_sems.at[2],
                recv_sem=dec_sems.at[3],
                device_id=(across, head),
                device_id_type=MESH,
            )
            dec_chip_copy.start()
        else:
            if h == 1:
                dec_chip_copy.wait()
            sum_pairs(h - 1)
        orthogonalize(h)
        if h == 0:
            arrive(4, (3, 4, 5))
    pl.when((group == 0) & (side == 1))(lambda: chain(0))
    sum_pairs(heads - 1)
    pl.when(side == 0)(lambda: arrive(2, (6, 8)))
    arrive(8, (7,))

    loads[5].wait()
    lane = lax.broadcasted_iota(jnp.int32, (rows, 256), 1)
    starts = [0, heads * dim - 256]
    for h in range(heads):
        begin = h * dim - starts[h]
        inside = (lane >= begin) & (lane < begin + dim)
        wide = q_ref[:, starts[h] : starts[h] + 256].astype(F32)
        qpad[h] = jnp.where(inside, wide, 0.0).astype(BF)
    acc[...] = jnp.zeros(acc.shape, F32)
    top[...] = jnp.full(top.shape, FAR, F32)
    total[...] = jnp.zeros(total.shape, F32)
    gap = lax.broadcasted_iota(jnp.int32, (rows, rows), 0) - lax.broadcasted_iota(
        jnp.int32, (rows, rows), 1
    )

    def attend(distance):
        slot = slot_of(distance)
        back = gap + distance * rows
        for h in range(heads):
            cols = slice(starts[h], starts[h] + 256)
            scores = dot1(qpad[h], kv[slot, 0, :, cols], NT) * scale
            if distance == 0:
                scores = jnp.where(back >= 0, scores, FAR)
            if distance == reach:
                scores = jnp.where(back < WINDOW, scores, FAR)
            old_top = top[h][:, 0:1]
            new_top = jnp.maximum(old_top, jnp.max(scores, axis=1, keepdims=True))
            weights = jnp.exp(scores - new_top)
            shrink = jnp.exp(old_top - new_top)
            total[h] = jnp.broadcast_to(
                total[h][:, 0:1] * shrink + jnp.sum(weights, axis=1, keepdims=True), (rows, 128)
            )
            acc[h] = acc[h] * shrink + dot1(weights.astype(BF), kv[slot, 1, :, cols])
            top[h] = jnp.broadcast_to(new_top, (rows, 128))

    def turn_of(distance):
        if distance % 2 == 1:
            await_block(distance)
        attend(distance)

    last_at = {0: 2, 1: 4, 2: 6}

    def rest():
        for h in range(1, heads):
            chain(h)

    for position, distance in enumerate((0, 1, 3, 2, 4, 8, 7, 5, 6)):
        if position == 6:
            arrive(6, (9,))
        if position in (2, 4, 6, 8) and position // 2 < n_group:
            pl.when((group == position // 2) & (side == 1))(lambda: chain(0))
        for g, at in last_at.items():
            if at == position:
                pl.when((group == g) & (side == 1))(rest)
        pl.when(me >= distance)(functools.partial(turn_of, distance))

    for h in range(heads):
        cols = slice(h * dim, (h + 1) * dim)
        begin = h * dim - starts[h]
        attended = acc[h][:, begin : begin + dim] / total[h][:, 0:1]
        share_attn[h] = rms_rows(attended) * again_ref[...].reshape(1, -1)[:, cols]
        query = q_ref[...].astype(F32)[:, cols]
        query_low[h] = query.astype(BF)
        query_scale[h] = jnp.broadcast_to(rms_inverse(query), (rows, 128))

    pl.when((group > 4) | (side == 0))(lambda: chain(0))

    pl.when((group > 2) & has_next & (side == 1))(rest)
    loads[6].wait()
    for h in range(heads):
        if h == 1:
            pl.when((side == 0) | ((group > 1) & (group + 1 == n_group)))(rest)
        for p in range(h * per_head, (h + 1) * per_head):
            h_copy(p).wait_recv()
            state[p // SPLIT, rows_at(p, other_at), :] = h_in[p].astype(F32)
        cols = slice(h * dim, (h + 1) * dim)
        query = query_low[h]
        scale_q = query_scale[h][:, 0:1]
        pre_gate = scale_q * dot2(query, halves(gate_ref[h] + state[3 * h]))
        pre_up = scale_q * dot2(query, halves(up_ref[h] + state[3 * h + 1]))
        hidden = pre_gate * jax.nn.sigmoid(pre_gate) * pre_up
        applied = dot3(halves(hidden), halves(downt[h] + state[3 * h + 2]), NT)
        mixed[h] = (
            rms_rows(applied) * tgain_ref[...].reshape(1, -1)[:, cols] + share_attn[h]
        ).astype(BF)

    share = rows // n_head

    def project(target):
        at = pl.multiple_of(target * share, share)
        result = dot1(mixed[0, pl.ds(at, share), :], proj_ref[0:dim, :])
        for h in range(1, heads):
            result = result + dot1(
                mixed[h, pl.ds(at, share), :], proj_ref[h * dim : (h + 1) * dim, :]
            )
        return result

    def p_copy(hop):
        return pltpu.make_async_remote_copy(
            src_ref=p_out.at[hop - 1],
            dst_ref=p_in.at[hop - 1],
            send_sem=p_send.at[hop - 1],
            recv_sem=p_recv.at[hop - 1],
            device_id=(me, lax.rem(head + hop, n_head)),
            device_id_type=MESH,
        )

    for hop in range(1, n_head):
        p_out[hop - 1] = project(lax.rem(head + hop, n_head)).astype(BF)
        p_copy(hop).start()
    result = project(head)
    for hop in range(1, n_head):
        p_copy(hop).wait_recv()
        result = result + p_in[hop - 1].astype(F32)
    out_ref[...] = result.astype(BF)

    for number, (cond, from_slot, to_slot, _, target) in enumerate(sends):

        @pl.when(cond)
        def _():
            kv_copy(
                jnp.maximum(from_slot, 0), jnp.maximum(to_slot, 0), number, target
            ).wait_send()

    for p in range(pieces):
        x_copy(p).wait_send()
        h_copy(p).wait_send()

        @pl.when(side == 0)
        def _():
            t_copy(p).wait_send()

        @pl.when((group > 0) & (side == 1))
        def _():
            y_copy(p).wait_send()

        @pl.when(has_next & (side == 1))
        def _():
            s_copy(p).wait_send()

    for hop in range(1, n_head):
        p_copy(hop).wait_send()


def local(
    n_seq,
    n_head,
    query_rows,
    key_rows,
    value_rows,
    rates,
    fw_decay,
    fw_step,
    fast_gate,
    fast_up,
    fast_down,
    ttt_gain,
    attn_gain,
    out_proj,
):
    rows, cols = query_rows.shape
    heads, dim, fast = fast_gate.shape
    width = out_proj.shape[1]
    share = rows // n_head
    mats = 3 * heads
    slots = WINDOW // rows + GROUP
    dma = pltpu.SemaphoreType.DMA
    pieces = mats * SPLIT
    chunk = dim // 2 // SPLIT
    piece = pltpu.VMEM((pieces, chunk, fast), BF)
    moved = pl.BlockSpec(memory_space=pl.ANY)
    small = pl.BlockSpec(memory_space=pltpu.VMEM)
    return pl.pallas_call(
        functools.partial(kernel, n_seq, n_head),
        out_shape=jax.ShapeDtypeStruct((share, width), BF),
        in_specs=[moved] * 3 + [small] * 3 + [moved] * 3 + [small] * 2 + [moved],
        out_specs=pl.BlockSpec(memory_space=pltpu.VMEM),
        scratch_shapes=[
            pltpu.VMEM((rows, cols), BF),
            pltpu.VMEM((heads, dim, fast), F32),
            pltpu.VMEM((heads, dim, fast), F32),
            pltpu.VMEM((heads, dim, fast), F32),
            pltpu.VMEM((cols, width), BF),
            pltpu.VMEM((slots, 2, rows, cols), BF),
            pltpu.VMEM((8, 128), F32),
            pltpu.VMEM((8, 128), F32),
            pltpu.VMEM((8, 128), F32),
            pltpu.VMEM((8, 128), F32),
            pltpu.VMEM((mats, dim, fast), F32),
            piece,
            piece,
            pltpu.VMEM((pieces, chunk, fast), F32),
            piece,
            piece,
            piece,
            piece,
            piece,
            piece,
            pltpu.VMEM((mats, dim, fast), F32),
            pltpu.VMEM((heads, rows, 256), BF),
            pltpu.VMEM((heads, rows, 256), F32),
            pltpu.VMEM((heads, rows, 128), F32),
            pltpu.VMEM((heads, rows, 128), F32),
            pltpu.VMEM((heads, rows, dim), F32),
            pltpu.VMEM((heads, rows, dim), BF),
            pltpu.VMEM((heads, rows, 128), F32),
            pltpu.VMEM((heads, rows, dim), BF),
            pltpu.VMEM((n_head - 1, share, width), BF),
            pltpu.VMEM((n_head - 1, share, width), BF),
            dma((7,)),
            dma((10,)),
            dma((slots,)),
            dma((4,)),
            dma((pieces,)),
            dma((pieces,)),
            dma((pieces,)),
            dma((pieces,)),
            dma((pieces,)),
            dma((pieces,)),
            dma((pieces,)),
            dma((pieces,)),
            dma((pieces,)),
            dma((n_head - 1,)),
            dma((n_head - 1,)),
        ],
        compiler_params=pltpu.CompilerParams(
            collective_id=0, has_side_effects=True, vmem_limit_bytes=56 * 1024 * 1024
        ),
    )(
        query_rows,
        key_rows,
        value_rows,
        rates.T,
        fw_decay,
        fw_step.reshape(1, -1),
        fast_gate,
        fast_up,
        jnp.swapaxes(fast_down, 1, 2),
        ttt_gain,
        attn_gain,
        out_proj,
    )


def solution(mesh):
    in_specs = (
        P("seq", "head"),
        P("seq", "head"),
        P("seq", "head"),
        P("seq", "head"),
        P("seq", "head"),
        P("head"),
        P("head", None, None),
        P("head", None, None),
        P("head", None, None),
        P("head"),
        P("head"),
        P("head", None),
    )
    out_specs = P(("seq", "head"), None)
    body = functools.partial(local, mesh.shape["seq"], mesh.shape["head"])
    return jax.shard_map(body, mesh=mesh, in_specs=in_specs, out_specs=out_specs, check_vma=False)
```
